128 devices in a mesh: wide: 16 (over y, x), narrow: 8 (over z, core).
Axes of the slice: x: 4, y: 4, z: 4, core: 2. Of those that a mesh axis runs over, the one named last changes fastest.
Arguments:
- features: bfloat16 [131072, 1024], P(('wide', 'narrow')), may hold values from -6 to 6
- cluster_ids: int32 [131072, 1], P(('wide', 'narrow')), may hold values from 0 to 511; in each aligned block of 8192 rows (0 to 8191, 8192 to 16383, ...) at most 32 rows name the same one
- cluster_slots: int32 [512], replicated, may hold values from 0 to 511, each once
- w_first: bfloat16 [1024, 1024], replicated, may hold values from -0.1875 to 0.1875
- w_second: bfloat16 [1024, 1024], replicated, may hold values from -0.1875 to 0.1875
- w_third: bfloat16 [1024, 1024], replicated, may hold values from -0.1875 to 0.1875
- emb_gain: float32 [1024], replicated, may hold values from 0.25 to 1.75
- queries: bfloat16 [64, 1024], P('wide', 'narrow'), may hold values from -0.1875 to 0.1875
Outputs:
- best_scores: float32 [64, 512], P('narrow', 'wide')
- index_slab: bfloat16 [16, 512, 32, 1024], P(None, 'wide', None, 'narrow')
The draws below stay inside these ranges and needn't reach their ends.
Inputs may be any that keep to these rules, and one draw needn't show every extreme that they name: `cluster_ids`: every cluster is named by some item. In each aligned block of 8 * 1024 rows no cluster is named by more than 32 rows, a bound that some block reaches. `cluster_slots`: each number once. Output columns k * 32 to (k + 1) * 32 - 1 belong to the clusters owned by index k of wide.
All inputs are finite; a program needn't handle non-finite values.
Results may differ from the reference program's by a relative error of at most 0.014.
Values may be sent and summed in bfloat16 or wider, within the bound.
A program may use at most 192 MiB of HBM per device.

```python
import math
import jax
import jax.numpy as jnp
import numpy as np
from jax import lax

F = 1024
H = 1024
E = 1024
ROWS_DEV = 1024
Q = 64
ITEMS = 131072
CLUSTERS = 512
MOST = 32
N_WIDE = 16
N_NARROW = 8


def level_of(stream_key, extent, shards, low, top_value):
    loudness, own = 1.0, jax.random.fold_in(stream_key, 6)
    for dim, parts in shards:
        heights = jnp.exp(jax.random.uniform(jax.random.fold_in(own, dim), (parts,), jnp.float32, low / len(shards), top_value / len(shards)))
        loudness = loudness * jnp.repeat(heights, extent[dim] // parts).reshape([-1 if axis == dim else 1 for axis in range(len(extent))])
    return loudness


def routed_block(rng, own, number, rows, count, top, limit, slope):
    sequence = jax.random.permutation(rng, count)
    crowded, usual = shares(count, rows * top, limit, slope, True), shares(count, rows * top, limit, slope, False)
    places = jnp.arange(count)

    def named(lengths, turn):
        used = int((lengths > 0).sum())
        fixed = max(1, used // 4)
        passed = fixed + (places - fixed + turn * (used - fixed)) % max(1, count - fixed)
        return jnp.zeros((count,), jnp.int32).at[sequence[jnp.where(places < fixed, places, passed)]].set(jnp.asarray(lengths, jnp.int32))

    lengths = jnp.where(number % 4 == 0, named(crowded, number // 4), named(usual, number - number // 4 - 1))
    mixed = jax.random.permutation(jax.random.fold_in(own, 3), count)
    donor, taker = mixed[0:count // 2 * 2:2], mixed[1:count // 2 * 2:2]
    room = jnp.minimum(lengths[donor] - 1, limit - lengths[taker]) // 2
    room = jnp.where((donor == sequence[0]) | (taker == sequence[0]) | (lengths[taker] == 0), 0, jnp.maximum(room, 0))
    passed = jax.random.randint(jax.random.fold_in(own, 4), (count // 2,), 0, 1 << 20) % (room + 1)
    lengths = lengths.at[donor].add(-passed).at[taker].add(passed)
    labels = jnp.searchsorted(jnp.cumsum(lengths), jnp.arange(rows * top), side="right").astype(jnp.int32)
    table = labels.reshape(top, rows).T
    table = table[jax.random.permutation(jax.random.fold_in(own, 1), rows)]
    turn = jax.random.randint(jax.random.fold_in(own, 2), (rows, 1), 0, top)
    return jnp.take_along_axis(table, (jnp.arange(top)[None, :] + turn) % top, axis=1)


def shares(amount, total, bound, lean, full):
    weights = [(1 << 20) // math.isqrt(grade ** lean) + 1 for grade in range(1, amount + 1)]
    largest = bound if full else min(bound, max(-(-total // amount), total * weights[0] // sum(weights)))
    least = 1 if total - largest >= amount - 1 else 0
    holding, spare = [largest] + [least] * (amount - 1), total - largest - least * (amount - 1)
    while spare > 0:
        candidates = [i for i in range(1, amount) if holding[i] < largest] or [i for i in range(1, amount) if holding[i] < bound]
        whole, remaining = sum([weights[i] for i in candidates]), spare
        for i in candidates:
            addition = min(bound - holding[i], max(1, remaining * weights[i] // whole), spare)
            holding[i] = holding[i] + addition
            spare = spare - addition
    return np.array(holding)


def gaussian(own_key, dims, width, most, shards=(), kind=jnp.bfloat16):
    drawn = width * jax.random.normal(own_key, dims, jnp.float32)
    if shards:
        drawn = drawn * level_of(own_key, dims, shards, -0.22, 0.18)
    return jnp.clip(drawn, -most, most).astype(kind)


def setup_inputs(seed: int = 0) -> dict:
    key_list = jax.random.split(jax.random.key(seed), 9)
    features = gaussian(key_list[0], (ITEMS, F), 1.0, 6.0, ((0, 128),))
    cluster_ids_keys = jax.random.split(jax.random.fold_in(key_list[1], 1), ITEMS // (N_NARROW * ROWS_DEV))
    cluster_ids_turns = jax.random.permutation(jax.random.fold_in(key_list[1], 3), ITEMS // (N_NARROW * ROWS_DEV))
    cluster_ids = jax.vmap(lambda own, number: routed_block(jax.random.fold_in(key_list[1], 2), own, number, N_NARROW * ROWS_DEV, CLUSTERS, 1, MOST, 2))(cluster_ids_keys, cluster_ids_turns).reshape((ITEMS, 1))
    cluster_slots = jax.random.permutation(key_list[2], CLUSTERS).astype(jnp.int32)
    w_first = gaussian(key_list[3], (F, H), F ** -0.5, 0.1875)
    w_second = gaussian(key_list[4], (H, H), H ** -0.5, 0.1875)
    w_third = gaussian(key_list[5], (H, E), H ** -0.5, 0.1875)
    emb_gain = jnp.clip(1.0 + 0.15 * jax.random.normal(key_list[6], (E,), jnp.float32), 0.25, 1.75)
    queries = gaussian(key_list[7], (Q, E), E ** -0.5, 0.1875, ((0, 16), (1, 8)))
    return dict(features=features, cluster_ids=cluster_ids, cluster_slots=cluster_slots, w_first=w_first, w_second=w_second, w_third=w_third, emb_gain=emb_gain, queries=queries)


def reference(features, cluster_ids, cluster_slots, w_first, w_second, w_third, emb_gain, queries):
    block_rows = N_NARROW * ROWS_DEV
    feats = features.reshape(N_WIDE, block_rows, F)
    ids = cluster_ids[:, 0].reshape(N_WIDE, block_rows)
    levels = jnp.arange(CLUSTERS, dtype=jnp.int32)

    def step(carry, inputs):
        block, block_ids = inputs
        first = jax.nn.silu(jnp.dot(block, w_first, preferred_element_type=jnp.float32)).astype(jnp.bfloat16)
        second = jax.nn.silu(jnp.dot(first, w_second, preferred_element_type=jnp.float32)).astype(jnp.bfloat16)
        raw = jnp.dot(second, w_third, preferred_element_type=jnp.float32)
        scale = lax.rsqrt(lax.optimization_barrier(jnp.mean(raw * raw, axis=1, keepdims=True)) + 1e-06)
        embedding = (raw * scale * emb_gain.astype(jnp.float32)).astype(jnp.bfloat16)
        score = jnp.dot(embedding, queries.T, preferred_element_type=jnp.float32)
        columns = jnp.take(cluster_slots, block_ids).astype(jnp.int32)
        best = jax.ops.segment_max(score, columns, num_segments=CLUSTERS)
        onehot = (block_ids[:, None] == levels[None, :]).astype(jnp.float32)
        ranks = lax.optimization_barrier(jnp.sum(onehot * (jnp.cumsum(onehot, axis=0) - 1.0), axis=1)).astype(jnp.int32)
        flat = (columns * MOST + ranks).astype(jnp.int32)
        slab = jnp.zeros((CLUSTERS * MOST, E), jnp.bfloat16).at[flat].set(embedding)
        return (jnp.maximum(carry, best), slab.reshape(CLUSTERS, MOST, E))
    start = jnp.full((CLUSTERS, Q), -jnp.inf, jnp.float32)
    final, slabs = lax.scan(step, start, (feats, ids))
    return (final.T, slabs)
```

```python
import functools
import math

import jax
import jax.numpy as jnp
from jax import lax
from jax.experimental import pallas as pl
from jax.experimental.pallas import tpu as pltpu
from jax.sharding import PartitionSpec as P

MESH = pl.DeviceIdType.MESH
CL_DEV = 32
MOST = 32
WIDE = 16
NARROW = 8
ROWS = 1024
PIECE = 128
SLOTS = 512
CHUNKS = 4
CHUNK = ROWS // CHUNKS
BLOCKS = NARROW * CHUNK // 128
CAP = 208
TAIL = CAP - 128
SELF = 2
NT = (((1,), (1,)), ((), ()))
F32 = jnp.float32
BF16 = jnp.bfloat16


def silu(v):
    half = 0.5 * v
    return half + half * jnp.tanh(half)


def loop(low, high, body):
    def step(i, carry):
        body(i)
        return carry

    lax.fori_loop(low, high, step, 0)


def peer_step(i):
    return i + (i + 13) // 15


def iota(shape, dim):
    return lax.broadcasted_iota(jnp.int32, shape, dim)


def exchange(
    feats_hbm, w1_hbm, w2_hbm, w3_hbm, gain_ref, ids_ref, slots_ref, query_ref,
    arrived_ref, tags_ref, best_ref,
    feats, w1, w2, w3, emb, land, rhs, stage, tag_out, ids_all, owner_of, levels, ranks, dest, dest_carry, spill,
    q_wide, q_mine, q_all, perm, ends, table, table_in, final, final_in,
    load_sem, ids_s, ids_r, qw_s, qw_r, qn_s, qn_r, emb_s, emb_r, data_s, data_r, tag_s, tag_r,
    table_s, table_r, final_s, final_r, own_sem,
):
    w = lax.axis_index("wide")
    n = lax.axis_index("narrow")

    def wide_peer(k):
        down = (2 + k) % 4
        across = (2 + k + k // 4) % 4
        return ((w // 4 + down) % 4) * 4 + (w % 4 + across) % 4

    def narrow_peer(d):
        return (n + d) % NARROW

    def remote(src, dst, send, recv, device):
        return pltpu.make_async_remote_copy(
            src_ref=src, dst_ref=dst, send_sem=send, recv_sem=recv, device_id=device, device_id_type=MESH
        )

    def ids_copy(d):
        return remote(ids_ref, ids_all.at[n], ids_s.at[d], ids_r.at[d], (w, narrow_peer(d)))

    def q_wide_copy(k):
        return remote(query_ref, q_wide.at[w], qw_s.at[k], qw_r.at[k], (wide_peer(k), n))

    def q_narrow_copy(d):
        return remote(q_mine, q_all.at[n], qn_s.at[d], qn_r.at[d], (w, narrow_peer(d)))

    def rows_of(c):
        return pl.ds(pl.multiple_of(c * CHUNK, CHUNK), CHUNK)

    def emb_copy(c, d):
        to = narrow_peer(d)
        return remote(
            emb.at[to, rows_of(c)], land.at[n, rows_of(c)], emb_s.at[c, d], emb_r.at[c, d], (w, to)
        )

    def slab_rows(c):
        return pl.ds(pl.multiple_of(c * CAP, 16), CAP)

    def data_copy(c, k):
        return remote(
            stage.at[c, k], arrived_ref.at[w, slab_rows(c)], data_s.at[c, k], data_r.at[c, k], (wide_peer(k), n)
        )

    def tag_copy(k):
        return remote(tag_out.at[k], tags_ref.at[w], tag_s.at[k], tag_r.at[k], (wide_peer(k), n))

    def table_copy(d):
        to = narrow_peer(d)
        return remote(table.at[to], table_in.at[n], table_s.at[d], table_r.at[d], (w, to))

    def final_copy(k):
        to = wide_peer(k)
        return remote(final.at[to], final_in.at[w], final_s.at[k], final_r.at[k], (to, n))

    def own_data(c):
        return pltpu.make_async_copy(stage.at[c, SELF], arrived_ref.at[w, slab_rows(c)], own_sem.at[c])

    def own_tag():
        return pltpu.make_async_copy(tag_out.at[SELF], tags_ref.at[w], own_sem.at[CHUNKS])

    loads = [
        pltpu.make_async_copy(src, dst, load_sem.at[i])
        for i, (src, dst) in enumerate(((feats_hbm, feats), (w1_hbm, w1), (w2_hbm, w2), (w3_hbm, w3)))
    ]
    for load in loads:
        load.start()

    barrier = pltpu.get_barrier_semaphore()

    def greet_wide(i):
        pl.semaphore_signal(barrier, inc=1, device_id=(wide_peer(peer_step(i)), n), device_id_type=MESH)

    def greet_narrow(d):
        pl.semaphore_signal(barrier, inc=1, device_id=(w, narrow_peer(d)), device_id_type=MESH)

    loop(1, NARROW, greet_narrow)
    loop(0, WIDE - 1, greet_wide)

    slot_level = iota((SLOTS, SLOTS), 0)
    cluster_level = iota((SLOTS, SLOTS), 1).astype(F32)
    holder = jnp.sum(jnp.where(slots_ref[...] == slot_level, cluster_level, 0.0), axis=1, keepdims=True)
    owner_of[...] = jnp.broadcast_to(holder, (SLOTS, 128)).astype(jnp.int32)
    place = (iota((SLOTS, 128), 0) % CL_DEV * MOST).astype(F32)
    levels[...] = place
    ranks[...] = jnp.zeros_like(ranks)
    dest_carry[...] = jnp.zeros_like(dest_carry)
    ids_all[n] = ids_ref[...]
    q_wide[w] = query_ref[...]

    pl.semaphore_wait(barrier, NARROW - 1 + WIDE - 1)
    loop(1, NARROW, lambda d: ids_copy(d).start())
    loop(0, WIDE - 1, lambda i: q_wide_copy(peer_step(i)).start())
    for load in loads:
        load.wait()

    def tower(c):
        x = feats[rows_of(c), :]
        first = silu(jnp.dot(x, w1[...], preferred_element_type=F32)).astype(BF16)
        second = silu(jnp.dot(first, w2[...], preferred_element_type=F32)).astype(BF16)
        raw = jnp.dot(second, w3[...], preferred_element_type=F32)
        scale = lax.rsqrt(jnp.mean(raw * raw, axis=1, keepdims=True) + 1e-06)
        embedding = (raw * scale * gain_ref[...]).astype(BF16)
        for j in range(NARROW):
            emb[j, rows_of(c), :] = embedding[:, j * PIECE : (j + 1) * PIECE]
        land[n, rows_of(c), :] = emb[n, rows_of(c), :]
        loop(1, NARROW, lambda d: emb_copy(c, d).start())

    def place_rows():
        loop(1, NARROW, lambda d: ids_copy(d).wait_recv())
        upto = iota((128, 256), 0) <= iota((128, 256), 1)
        sums = upto.astype(F32).astype(BF16)

        def source(m):
            for k in range(8):
                c = k * 128 // CHUNK
                q = m * (CHUNK // 128) + k % (CHUNK // 128)
                row = ids_all[m, k : k + 1, :]
                named = owner_of[...] == row
                onehot = jnp.where(named, 1.0, 0.0)
                counts = jnp.dot(onehot.astype(BF16), sums, preferred_element_type=F32)
                where = jnp.where(named, counts[:, :128] + levels[...], 0.0)
                ranks[c, pl.ds(q, 1), :] = jnp.sum(where, axis=0, keepdims=True)
                levels[...] += counts[:, 128:]
                owned = jnp.sum(onehot.reshape(WIDE, CL_DEV, 128), axis=1)
                ordered = jnp.dot(owned.astype(BF16), sums, preferred_element_type=F32)
                dest[c, q] = jnp.where(owned > 0.0, ordered[:, :128] + dest_carry[c] - 1.0, -1.0)
                dest_carry[c] += ordered[:, 128:]

        loop(0, NARROW, source)
        most = jnp.max(dest_carry[...].reshape(CHUNKS * WIDE, 128), axis=0, keepdims=True)
        spill[...] = jnp.broadcast_to(jnp.where(most > float(CAP), 1.0, 0.0), spill.shape)

        loop(0, WIDE - 1, lambda i: q_wide_copy(peer_step(i)).wait_recv())
        at = iota((4 * WIDE, 8 * WIDE), 0)
        pick = iota((4 * WIDE, 8 * WIDE), 1) == at // 4 * 8 + at % 4
        spread = q_wide[...].reshape(8 * WIDE, PIECE).astype(BF16)
        q_mine[...] = jnp.dot(pick.astype(F32).astype(BF16), spread, preferred_element_type=F32).astype(BF16)
        q_all[n] = q_mine[...]
        loop(1, NARROW, lambda d: q_narrow_copy(d).start())

    def pack(c):
        loop(1, NARROW, lambda d: emb_copy(c, d).wait_recv())
        turned = jnp.transpose(ranks[c])
        left = iota((128, 128), 1) < 64
        for q in range(BLOCKS):
            m, part = q // (CHUNK // 128), q % (CHUNK // 128)
            start = pl.multiple_of(c * CHUNK + part * 128, 128)
            rhs[q * 128 : (q + 1) * 128, 0:128] = land[m, pl.ds(start, 128), :]
            column = jnp.broadcast_to(turned[:, q : q + 1], (128, 128))
            high = jnp.floor(column * (1.0 / 32.0)) * 32.0
            rhs[q * 128 : (q + 1) * 128, 128:256] = jnp.where(left, high, column - high).astype(BF16)

        spot = iota((CAP, 128), 0).astype(F32)
        eye = iota((128, 128), 0) == iota((128, 128), 1)
        eye_tail = iota((TAIL, 128), 0) == iota((TAIL, 128), 1)
        last_lane = iota((1, 128), 1) == 127

        def to_owner(k):
            to = wide_peer(k)
            parts = []
            for q in range(BLOCKS):
                row = dest[c, q, pl.ds(to, 1), :]
                parts.append(jnp.where(spot == row, 1.0, 0.0).astype(BF16))
            onehot = jnp.concatenate(parts, axis=1)
            packed = jnp.dot(onehot, rhs[...], preferred_element_type=F32)
            stage[c, k] = packed[:, :128].astype(BF16)
            tag = packed[:, 128:]
            tag = tag + pltpu.roll(tag, 64, 1)
            upper = jnp.sum(jnp.where(eye, tag[:128], 0.0), axis=0, keepdims=True)
            lower = jnp.sum(jnp.where(eye_tail, tag[128:], 0.0), axis=0, keepdims=True)
            tag_out[k, pl.ds(2 * c, 1), :] = upper
            tag_out[k, pl.ds(2 * c + 1, 1), :] = lower + jnp.where(last_lane, spill[0:1, :], 0.0)

            @pl.when(k != SELF)
            def _():
                data_copy(c, k).start()

                @pl.when(c == CHUNKS - 1)
                def _():
                    tag_copy(k).start()

            @pl.when(k == SELF)
            def _():
                own_data(c).start()

                @pl.when(c == CHUNKS - 1)
                def _():
                    own_tag().start()

        loop(0, WIDE, to_owner)

    def turn(t):
        @pl.when(t < CHUNKS)
        def _():
            tower(t)

        @pl.when(t == 0)
        def _():
            place_rows()

        @pl.when(t >= 1)
        def _():
            pack(t - 1)

    loop(0, CHUNKS + 1, turn)

    loop(1, NARROW, lambda d: q_narrow_copy(d).wait_recv())
    score = jnp.zeros((4 * WIDE, ROWS), F32)
    for j in range(NARROW):
        score += lax.dot_general(q_all[j], emb[j], NT, preferred_element_type=F32)
    ids_f = ids_ref[...].astype(F32)
    id_row = jnp.concatenate([ids_f[k : k + 1, :] for k in range(8)], axis=1)
    key_row = id_row * float(ROWS) + iota((1, ROWS), 1).astype(F32)
    eye = iota((128, 128), 0) == iota((128, 128), 1)
    order = iota((128, ROWS), 1).astype(F32)
    for k in range(8):
        key = jnp.sum(jnp.where(eye, key_row[:, k * 128 : (k + 1) * 128], 0.0), axis=1, keepdims=True)
        position = jnp.sum(jnp.where(key_row < key, 1.0, 0.0), axis=1, keepdims=True)
        perm[k * 128 : (k + 1) * 128, :] = jnp.where(order == position, 1.0, 0.0).astype(BF16)
    high = score.astype(BF16)
    low = (score - high.astype(F32)).astype(BF16)
    id_high = jnp.floor(id_row * (1.0 / 32.0)) * 32.0
    line = iota((16, ROWS), 0)
    extra = jnp.where(line == 0, id_high, jnp.where(line == 1, id_row - id_high, 0.0)).astype(BF16)
    arranged = jnp.dot(jnp.concatenate([high, low, extra], axis=0), perm[...], preferred_element_type=F32)
    top = arranged[0:64] + arranged[64:128]
    seg = jnp.broadcast_to(arranged[128:129] + arranged[129:130], (8, ROWS))
    lane = iota((8, ROWS), 1)
    for step in (1, 2, 4, 8, 16):
        same = (pltpu.roll(seg, step, 1) == seg) & (lane >= step)
        gate = jnp.where(same, 0.0, -jnp.inf)[0:1]
        top = jnp.maximum(top, pltpu.roll(top, step, 1) + gate)
    closing = (pltpu.roll(seg, ROWS - 1, 1) != seg) | (lane == ROWS - 1)
    end_id = jnp.where(closing, seg, -1.0)[0:1]
    for k in range(ROWS // 128):
        match = owner_of[...].astype(F32) == end_id[:, k * 128 : (k + 1) * 128]
        ends[:, k * 128 : (k + 1) * 128] = jnp.where(match, 1.0, 0.0).astype(BF16)
    high = top.astype(BF16)
    low = (top - high.astype(F32)).astype(BF16)
    ones = jnp.ones((16, ROWS), BF16)
    found = lax.dot_general(jnp.concatenate([high, low, ones], axis=0), ends[...], NT, preferred_element_type=F32)
    by_slot = jnp.where(found[128:129] > 0.0, found[0:64] + found[64:128], -jnp.inf)
    for j in range(NARROW):
        table[j] = by_slot[8 * j : 8 * j + 8]
    table_in[n] = table[n]
    loop(1, NARROW, lambda d: table_copy(d).start())
    loop(1, NARROW, lambda d: table_copy(d).wait_recv())
    merged = jnp.max(table_in[...], axis=0)
    for o in range(WIDE):
        group = merged[:, o // 4 * 128 : o // 4 * 128 + 128]
        final[o] = pltpu.roll(group, (128 - 32 * (o % 4)) % 128, 1) if o % 4 else group
    final_in[w] = final[w]
    loop(0, WIDE - 1, lambda i: final_copy(peer_step(i)).start())
    loop(0, WIDE - 1, lambda i: final_copy(peer_step(i)).wait_recv())
    best_ref[...] = jnp.max(final_in[...], axis=0)

    def settle_wide(i):
        k = peer_step(i)
        q_wide_copy(k).wait_send()
        final_copy(k).wait_send()
        tag_copy(k).wait()

    def settle_narrow(d):
        ids_copy(d).wait_send()
        q_narrow_copy(d).wait_send()
        table_copy(d).wait_send()

    loop(0, WIDE - 1, settle_wide)
    loop(1, NARROW, settle_narrow)

    def settle_chunk(c):
        loop(1, NARROW, lambda d: emb_copy(c, d).wait_send())
        loop(0, WIDE - 1, lambda i: data_copy(c, peer_step(i)).wait())
        own_data(c).wait()

    loop(0, CHUNKS, settle_chunk)
    own_tag().wait()


def run_exchange(features, w_first, w_second, w_third, gain, ids, slots, queries):
    vmem = pl.BlockSpec(memory_space=pltpu.VMEM)
    anywhere = pl.BlockSpec(memory_space=pl.ANY)
    dma = pltpu.SemaphoreType.DMA
    return pl.pallas_call(
        exchange,
        out_shape=(
            jax.ShapeDtypeStruct((WIDE, CHUNKS * CAP, PIECE), BF16),
            jax.ShapeDtypeStruct((WIDE, 8, 128), F32),
            jax.ShapeDtypeStruct((8, 128), F32),
        ),
        in_specs=[anywhere] * 4 + [vmem] * 4,
        out_specs=(anywhere, anywhere, vmem),
        scratch_shapes=[
            pltpu.VMEM((ROWS, 1024), BF16),
            pltpu.VMEM((1024, 1024), BF16),
            pltpu.VMEM((1024, 1024), BF16),
            pltpu.VMEM((1024, 1024), BF16),
            pltpu.VMEM((NARROW, ROWS, PIECE), BF16),
            pltpu.VMEM((NARROW, ROWS, PIECE), BF16),
            pltpu.VMEM((NARROW * CHUNK, 256), BF16),
            pltpu.VMEM((CHUNKS, WIDE, CAP, PIECE), BF16),
            pltpu.VMEM((WIDE, 8, 128), F32),
            pltpu.VMEM((NARROW, 8, 128), jnp.int32),
            pltpu.VMEM((SLOTS, 128), jnp.int32),
            pltpu.VMEM((SLOTS, 128), F32),
            pltpu.VMEM((CHUNKS, 128, 128), F32),
            pltpu.VMEM((CHUNKS, BLOCKS, WIDE, 128), F32),
            pltpu.VMEM((CHUNKS, WIDE, 128), F32),
            pltpu.VMEM((8, 128), F32),
            pltpu.VMEM((WIDE, 8, PIECE), F32),
            pltpu.VMEM((4 * WIDE, PIECE), BF16),
            pltpu.VMEM((NARROW, 4 * WIDE, PIECE), BF16),
            pltpu.VMEM((ROWS, ROWS), BF16),
            pltpu.VMEM((SLOTS, ROWS), BF16),
            pltpu.VMEM((NARROW, 8, SLOTS), F32),
            pltpu.VMEM((NARROW, 8, SLOTS), F32),
            pltpu.VMEM((WIDE, 8, 128), F32),
            pltpu.VMEM((WIDE, 8, 128), F32),
            dma((4,)),
            dma((NARROW,)), dma((NARROW,)),
            dma((WIDE,)), dma((WIDE,)),
            dma((NARROW,)), dma((NARROW,)),
            dma((CHUNKS, NARROW)), dma((CHUNKS, NARROW)),
            dma((CHUNKS, WIDE)), dma((CHUNKS, WIDE)),
            dma((WIDE,)), dma((WIDE,)),
            dma((NARROW,)), dma((NARROW,)),
            dma((WIDE,)), dma((WIDE,)),
            dma((CHUNKS + 1,)),
        ],
        compiler_params=pltpu.CompilerParams(
            collective_id=0, has_side_effects=True, vmem_limit_bytes=56 * 2**20
        ),
        name="exchange",
    )(features, w_first, w_second, w_third, gain, ids, slots, queries)


def unpack(arrived_ref, tags_ref, slab_ref):
    spot = iota((CL_DEV * MOST, 1), 0).astype(F32) + 1.0
    total = jnp.zeros((CL_DEV * MOST, PIECE), F32)
    for c in range(CHUNKS):
        row = jnp.concatenate([tags_ref[0, 2 * c : 2 * c + 1, :], tags_ref[0, 2 * c + 1 : 2 * c + 2, :TAIL]], axis=1)
        onehot = jnp.where(spot == row, 1.0, 0.0).astype(BF16)
        total += jnp.dot(onehot, arrived_ref[0, c * CAP : (c + 1) * CAP, :], preferred_element_type=F32)
    slab_ref[0] = total.astype(BF16)


def run_unpack(arrived, tags):
    return pl.pallas_call(
        unpack,
        grid=(WIDE,),
        out_shape=jax.ShapeDtypeStruct((WIDE, CL_DEV * MOST, PIECE), BF16),
        in_specs=[
            pl.BlockSpec((1, CHUNKS * CAP, PIECE), lambda b: (b, 0, 0)),
            pl.BlockSpec((1, 8, 128), lambda b: (b, 0, 0)),
        ],
        out_specs=pl.BlockSpec((1, CL_DEV * MOST, PIECE), lambda b: (b, 0, 0)),
        compiler_params=pltpu.CompilerParams(vmem_limit_bytes=32 * 2**20),
        name="unpack",
    )(arrived, tags)


def slot_table(id_list, cluster_slots, total):
    levels = jnp.arange(total, dtype=jnp.int32)
    onehot = (id_list[:, None] == levels[None, :]).astype(jnp.bfloat16)
    high_part = (cluster_slots // 64).astype(jnp.bfloat16)
    low_part = (cluster_slots % 64).astype(jnp.bfloat16)
    slot_value = 64.0 * jnp.dot(onehot, high_part, preferred_element_type=jnp.float32) + jnp.dot(
        onehot, low_part, preferred_element_type=jnp.float32
    )
    return (onehot, slot_value.astype(jnp.int32))


def cluster_ranks(onehot):
    count, total = onehot.shape
    block = math.gcd(count, 256)
    number = count // block
    stacked = onehot.reshape(number, block, total)
    inner = jnp.arange(block, dtype=jnp.int32)
    lower = (inner[:, None] >= inner[None, :]).astype(jnp.bfloat16)
    inside = jnp.einsum("rs,bsc->brc", lower, stacked, preferred_element_type=jnp.float32)
    block_sums = inside[:, -1, :]
    outer = jnp.arange(number, dtype=jnp.int32)
    before = (outer[:, None] > outer[None, :]).astype(jnp.float32)
    earlier = jnp.dot(
        before, block_sums, precision=lax.Precision.HIGHEST, preferred_element_type=jnp.float32
    )
    position = jnp.sum(stacked * (inside - 1.0 + earlier[:, None, :]), axis=2)
    return (position.reshape(count).astype(jnp.int32), jnp.sum(block_sums, axis=0))


def padded_slab(features, cluster_ids, cluster_slots, w_first, w_second, w_third, emb_gain):
    first = jax.nn.silu(jnp.dot(features, w_first, preferred_element_type=F32)).astype(BF16)
    second = jax.nn.silu(jnp.dot(first, w_second, preferred_element_type=F32)).astype(BF16)
    raw = jnp.dot(second, w_third, preferred_element_type=F32)
    scale = lax.rsqrt(jnp.mean(raw * raw, axis=1, keepdims=True) + 1e-06)
    embedding = (raw * scale * emb_gain).astype(BF16)
    block_ids = lax.all_gather(cluster_ids[:, 0], "narrow", axis=0, tiled=True)
    block_rows = block_ids.shape[0]
    onehot, slot_of = slot_table(block_ids, cluster_slots, SLOTS)
    positions, _ = cluster_ranks(onehot)
    flat_slot = slot_of * MOST + positions
    sliced = lax.all_to_all(embedding, "narrow", split_axis=1, concat_axis=0, tiled=True)
    source = (
        jnp.full((SLOTS * MOST,), block_rows, jnp.int32)
        .at[flat_slot]
        .set(jnp.arange(block_rows, dtype=jnp.int32))
    )
    padded = jnp.concatenate([sliced, jnp.zeros((1, PIECE), BF16)], axis=0)
    outgoing = jnp.take(padded, source, axis=0).reshape(WIDE, CL_DEV * MOST, PIECE)
    return lax.all_to_all(outgoing, "wide", split_axis=0, concat_axis=0, tiled=True)


def shards(features, cluster_ids, cluster_slots, w_first, w_second, w_third, emb_gain, queries):
    ids = cluster_ids.reshape(8, 128)
    query = jnp.pad(queries.astype(F32), ((0, 4), (0, 0)))
    arrived, tags, best = run_exchange(
        features, w_first, w_second, w_third, emb_gain.reshape(1, 1024), ids, cluster_slots.reshape(1, SLOTS), query
    )
    fits = jnp.max(tags[:, 7, 127]) == 0.0
    slab = lax.cond(
        fits,
        lambda: run_unpack(arrived, tags),
        lambda: padded_slab(features, cluster_ids, cluster_slots, w_first, w_second, w_third, emb_gain),
    )
    return (best[:, :CL_DEV], slab.reshape(WIDE, CL_DEV, MOST, PIECE))


def solution(mesh):
    placed = (
        P(("wide", "narrow"), None),
        P(("wide", "narrow"), None),
        P(),
        P(),
        P(),
        P(),
        P(),
        P("wide", "narrow"),
    )
    return jax.shard_map(
        shards,
        mesh=mesh,
        in_specs=placed,
        out_specs=(P("narrow", "wide"), P(None, "wide", None, "narrow")),
        check_vma=False,
    )
```

```python
import functools
import math

import jax
import jax.numpy as jnp
from jax import lax
from jax.experimental import pallas as pl
from jax.experimental.pallas import tpu as pltpu
from jax.sharding import PartitionSpec as P

MESH = pl.DeviceIdType.MESH
CL_DEV = 32
MOST = 32
WIDE = 16
NARROW = 8
ROWS = 1024
PIECE = 128
SLOTS = 512
SIZES = (256, 256, 256, 256)
CAPS = (176, 176, 176, 176, 48)
CHUNKS = len(SIZES)
GROUPS = CHUNKS + 1
STARTS = tuple(sum(SIZES[:c]) for c in range(CHUNKS))
OFFSETS = tuple(sum(CAPS[:g]) for g in range(GROUPS))
TOTAL = sum(CAPS)
BLOCKS = NARROW * ROWS // 128
SELF = 2
BATCH = 4
NT = (((1,), (1,)), ((), ()))
F32 = jnp.float32
BF16 = jnp.bfloat16


def silu(v):
    half = 0.5 * v
    return half + half * jnp.tanh(half)


def loop(low, high, body):
    def step(i, carry):
        body(i)
        return carry

    lax.fori_loop(low, high, step, 0)


def peer_step(i):
    return i + (i + 13) // 15


def iota(shape, dim):
    return lax.broadcasted_iota(jnp.int32, shape, dim)


def exchange(
    feats_hbm, w1_hbm, w2_hbm, w3_hbm, gain_ref, ids_ref, slots_ref, query_ref,
    arrived_ref, tags_ref, best_ref,
    feats, w1, w2, w3, emb, rhs, stage, tag_out, ids_all, owner_of, levels, ranks, dest, dest_over, dest_carry, spill, over_sum,
    q_wide, q_mine, q_all, perm, ends, table, table_in, final, final_in,
    load_sem, ids_s, ids_r, qw_s, qw_r, qn_s, qn_r, emb_s, emb_r, data_s, data_r, tag_s, tag_r,
    table_s, table_r, final_s, final_r, own_sem, own_tag_sem,
):
    w = lax.axis_index("wide")
    n = lax.axis_index("narrow")

    def wide_peer(k):
        down = (2 + k) % 4
        across = (2 + k + k // 4) % 4
        return ((w // 4 + down) % 4) * 4 + (w % 4 + across) % 4

    def narrow_peer(d):
        return (n + d) % NARROW

    def remote(src, dst, send, recv, device):
        return pltpu.make_async_remote_copy(
            src_ref=src, dst_ref=dst, send_sem=send, recv_sem=recv, device_id=device, device_id_type=MESH
        )

    def ids_copy(d):
        return remote(ids_ref, ids_all.at[n], ids_s.at[d], ids_r.at[d], (w, narrow_peer(d)))

    def q_wide_copy(k):
        return remote(query_ref, q_wide.at[w], qw_s.at[k], qw_r.at[k], (wide_peer(k), n))

    def q_narrow_copy(d):
        return remote(q_mine, q_all.at[n], qn_s.at[d], qn_r.at[d], (w, narrow_peer(d)))

    def rows_of(c):
        return pl.ds(STARTS[c], SIZES[c])

    def landing(c, m):
        start = NARROW * STARTS[c] + m * SIZES[c]
        return rhs.at[pl.ds(pl.multiple_of(start, 128), SIZES[c]), pl.ds(0, 128)]

    def emb_copy(c, d):
        to = narrow_peer(d)
        return remote(emb.at[to, rows_of(c)], landing(c, n), emb_s.at[c, d], emb_r.at[c, d], (w, to))

    def packed_rows(g):
        return pl.ds(OFFSETS[g], CAPS[g])

    def data_copy(g, k):
        return remote(
            stage.at[k, packed_rows(g)], arrived_ref.at[w, packed_rows(g)],
            data_s.at[g, k], data_r.at[g, k], (wide_peer(k), n),
        )

    def tag_copy(g, k):
        return remote(tag_out.at[k, g], tags_ref.at[w, g], tag_s.at[g, k], tag_r.at[g, k], (wide_peer(k), n))

    def table_copy(d):
        to = narrow_peer(d)
        return remote(table.at[to], table_in.at[n], table_s.at[d], table_r.at[d], (w, to))

    def final_copy(k):
        to = wide_peer(k)
        return remote(final.at[to], final_in.at[w], final_s.at[k], final_r.at[k], (to, n))

    def own_data(g):
        return pltpu.make_async_copy(
            stage.at[SELF, packed_rows(g)], arrived_ref.at[w, packed_rows(g)], own_sem.at[g]
        )

    def own_tag(g):
        return pltpu.make_async_copy(tag_out.at[SELF, g], tags_ref.at[w, g], own_tag_sem.at[g])

    loads = [
        pltpu.make_async_copy(src, dst, load_sem.at[i])
        for i, (src, dst) in enumerate(((feats_hbm, feats), (w1_hbm, w1), (w2_hbm, w2), (w3_hbm, w3)))
    ]
    for load in loads:
        load.start()

    barrier = pltpu.get_barrier_semaphore()

    def greet_wide(i):
        pl.semaphore_signal(barrier, inc=1, device_id=(wide_peer(peer_step(i)), n), device_id_type=MESH)

    def greet_narrow(d):
        pl.semaphore_signal(barrier, inc=1, device_id=(w, narrow_peer(d)), device_id_type=MESH)

    loop(1, NARROW, greet_narrow)
    loop(0, WIDE - 1, greet_wide)

    slot_level = iota((SLOTS, SLOTS), 0)
    cluster_level = iota((SLOTS, SLOTS), 1).astype(F32)
    holder = jnp.sum(jnp.where(slots_ref[...] == slot_level, cluster_level, 0.0), axis=1, keepdims=True)
    owner_of[...] = jnp.broadcast_to(holder, (SLOTS, 128)).astype(jnp.int32)
    place = (iota((SLOTS, 128), 0) % CL_DEV * MOST).astype(F32)
    levels[...] = place
    ranks[...] = jnp.zeros_like(ranks)
    dest_carry[...] = jnp.zeros_like(dest_carry)
    ids_all[n] = ids_ref[...]
    q_wide[w] = query_ref[...]

    def tower(c):
        x = feats[rows_of(c), :]
        first = silu(jnp.dot(x, w1[...], preferred_element_type=F32)).astype(BF16)
        second = silu(jnp.dot(first, w2[...], preferred_element_type=F32)).astype(BF16)
        raw = jnp.dot(second, w3[...], preferred_element_type=F32)
        scale = lax.rsqrt(jnp.mean(raw * raw, axis=1, keepdims=True) + 1e-06)
        embedding = (raw * scale * gain_ref[...]).astype(BF16)
        for j in range(NARROW):
            emb[j, rows_of(c), :] = embedding[:, j * PIECE : (j + 1) * PIECE]
        start = pl.multiple_of(NARROW * STARTS[c] + n * SIZES[c], 128)
        rhs[pl.ds(start, SIZES[c]), 0:128] = emb[n, rows_of(c), :]
    def send_rows(c):
        loop(1, NARROW, lambda d: emb_copy(c, d).start())

    def place_rows():
        loop(1, NARROW, lambda d: ids_copy(d).wait_recv())
        upto = iota((128, 256), 0) <= iota((128, 256), 1)
        sums = upto.astype(F32).astype(BF16)

        def source(m):
            for c in range(CHUNKS):
                for part in range(SIZES[c] // 128):
                    k = STARTS[c] // 128 + part
                    q = NARROW * STARTS[c] // 128 + m * (SIZES[c] // 128) + part
                    row = ids_all[m, k : k + 1, :]
                    named = owner_of[...] == row
                    onehot = jnp.where(named, 1.0, 0.0)
                    counts = jnp.dot(onehot.astype(BF16), sums, preferred_element_type=F32)
                    where = jnp.where(named, counts[:, :128] + levels[...], 0.0)
                    ranks[pl.ds(q, 1), :] = jnp.sum(where, axis=0, keepdims=True)
                    levels[...] += counts[:, 128:]
                    owned = jnp.sum(onehot.reshape(WIDE, CL_DEV, 128), axis=1)
                    ordered = jnp.dot(owned.astype(BF16), sums, preferred_element_type=F32)
                    dest[q] = jnp.where(owned > 0.0, ordered[:, :128] + dest_carry[c] - 1.0, -1.0)
                    dest_carry[c] += ordered[:, 128:]

        loop(0, NARROW, source)

        before = jnp.zeros((WIDE, 128), F32)
        for c in range(CHUNKS):
            shift = before - float(CAPS[c])
            first_block = NARROW * STARTS[c] // 128

            def beyond(i):
                q = first_block + i
                spot = dest[q]
                dest_over[q] = jnp.where(spot >= float(CAPS[c]), spot + shift, -1.0)

            loop(0, NARROW * SIZES[c] // 128, beyond)
            before = before + jnp.maximum(dest_carry[c] - float(CAPS[c]), 0.0)
        most = jnp.max(before, axis=0, keepdims=True)
        spill[...] = jnp.broadcast_to(jnp.where(most > float(CAPS[CHUNKS]), 1.0, 0.0), spill.shape)

        turned = jnp.transpose(ranks[...])
        left = iota((128, 128), 1) < 64
        for q in range(BLOCKS):
            column = jnp.broadcast_to(turned[:, q : q + 1], (128, 128))
            high = jnp.floor(column * (1.0 / 32.0)) * 32.0
            rhs[q * 128 : (q + 1) * 128, 128:256] = jnp.where(left, high, column - high).astype(BF16)

    def spread_queries():
        loop(0, WIDE - 1, lambda i: q_wide_copy(peer_step(i)).wait_recv())
        at = iota((4 * WIDE, 8 * WIDE), 0)
        pick = iota((4 * WIDE, 8 * WIDE), 1) == at // 4 * 8 + at % 4
        spread = q_wide[...].reshape(8 * WIDE, PIECE).astype(BF16)
        q_mine[...] = jnp.dot(pick.astype(F32).astype(BF16), spread, preferred_element_type=F32).astype(BF16)
        q_all[n] = q_mine[...]
        loop(1, NARROW, lambda d: q_narrow_copy(d).start())

    def write_tag(k, g, tag, cap):
        tag = tag + pltpu.roll(tag, 64, 1)
        for half in range(2):
            size = min(cap - 128 * half, 128)
            if size > 0:
                eye = iota((size, 128), 0) == iota((size, 128), 1)
                line = jnp.sum(jnp.where(eye, tag[128 * half : 128 * half + size], 0.0), axis=0, keepdims=True)
            else:
                line = spill[0:1, :]
            tag_out[k, g, half : half + 1, :] = line

    def send_group(k, g):
        @pl.when(k != SELF)
        def _():
            data_copy(g, k).start()
            tag_copy(g, k).start()

        @pl.when(k == SELF)
        def _():
            own_data(g).start()
            own_tag(g).start()

    def pack(c):
        loop(1, NARROW, lambda d: emb_copy(c, d).wait_recv())
        low_block, blocks = NARROW * STARTS[c] // 128, NARROW * SIZES[c] // 128
        cap, over = CAPS[c], CAPS[CHUNKS]
        both = cap + over
        spot = iota((cap, 128), 0).astype(F32)
        spot_over = iota((over, 128), 0).astype(F32)

        def to_owners(i):
            lines = []
            for j in range(BATCH):
                to = wide_peer(BATCH * i + j)
                for spots, level in ((dest, spot), (dest_over, spot_over)):
                    parts = []
                    for q in range(blocks):
                        row = spots[low_block + q, pl.ds(to, 1), :]
                        parts.append(jnp.where(level == row, 1.0, 0.0).astype(BF16))
                    lines.append(jnp.concatenate(parts, axis=1))
            onehot = jnp.concatenate(lines, axis=0)
            source = rhs[low_block * 128 : (low_block + blocks) * 128, :]
            packed = jnp.dot(onehot, source, preferred_element_type=F32)
            for j in range(BATCH):
                k = BATCH * i + j
                main = packed[both * j : both * j + cap]
                stage[k, packed_rows(c), :] = main[:, :128].astype(BF16)
                write_tag(k, c, main[:, 128:], cap)
                send_group(k, c)
                rest = packed[both * j + cap : both * (j + 1)]
                if c > 0:
                    rest = rest + over_sum[k]
                if c < CHUNKS - 1:
                    over_sum[k] = rest
                else:
                    stage[k, packed_rows(CHUNKS), :] = rest[:, :128].astype(BF16)
                    write_tag(k, CHUNKS, rest[:, 128:], over)
                    send_group(k, CHUNKS)

        loop(0, WIDE // BATCH, to_owners)

    def local_best():
        loop(1, NARROW, lambda d: q_narrow_copy(d).wait_recv())
        score = jnp.zeros((4 * WIDE, ROWS), F32)
        for j in range(NARROW):
            score += lax.dot_general(q_all[j], emb[j], NT, preferred_element_type=F32)
        ids_f = ids_ref[...].astype(F32)
        id_row = jnp.concatenate([ids_f[k : k + 1, :] for k in range(8)], axis=1)
        key_row = id_row * float(ROWS) + iota((1, ROWS), 1).astype(F32)
        eye = iota((128, 128), 0) == iota((128, 128), 1)
        order = iota((128, ROWS), 1).astype(F32)
        for k in range(8):
            key = jnp.sum(jnp.where(eye, key_row[:, k * 128 : (k + 1) * 128], 0.0), axis=1, keepdims=True)
            position = jnp.sum(jnp.where(key_row < key, 1.0, 0.0), axis=1, keepdims=True)
            perm[k * 128 : (k + 1) * 128, :] = jnp.where(order == position, 1.0, 0.0).astype(BF16)
        high = score.astype(BF16)
        low = (score - high.astype(F32)).astype(BF16)
        id_high = jnp.floor(id_row * (1.0 / 32.0)) * 32.0
        line = iota((16, ROWS), 0)
        extra = jnp.where(line == 0, id_high, jnp.where(line == 1, id_row - id_high, 0.0)).astype(BF16)
        arranged = jnp.dot(jnp.concatenate([high, low, extra], axis=0), perm[...], preferred_element_type=F32)
        top = arranged[0:64] + arranged[64:128]
        seg = jnp.broadcast_to(arranged[128:129] + arranged[129:130], (8, ROWS))
        lane = iota((8, ROWS), 1)
        for step in (1, 2, 4, 8, 16):
            same = (pltpu.roll(seg, step, 1) == seg) & (lane >= step)
            gate = jnp.where(same, 0.0, -jnp.inf)[0:1]
            top = jnp.maximum(top, pltpu.roll(top, step, 1) + gate)
        closing = (pltpu.roll(seg, ROWS - 1, 1) != seg) | (lane == ROWS - 1)
        end_id = jnp.where(closing, seg, -1.0)[0:1]
        for k in range(ROWS // 128):
            match = owner_of[...].astype(F32) == end_id[:, k * 128 : (k + 1) * 128]
            ends[:, k * 128 : (k + 1) * 128] = jnp.where(match, 1.0, 0.0).astype(BF16)
        high = top.astype(BF16)
        low = (top - high.astype(F32)).astype(BF16)
        ones = jnp.ones((16, ROWS), BF16)
        found = lax.dot_general(jnp.concatenate([high, low, ones], axis=0), ends[...], NT, preferred_element_type=F32)
        by_slot = jnp.where(found[128:129] > 0.0, found[0:64] + found[64:128], -jnp.inf)
        for j in range(NARROW):
            table[j] = by_slot[8 * j : 8 * j + 8]
        table_in[n] = table[n]
        loop(1, NARROW, lambda d: table_copy(d).start())

    def merge_narrow():
        loop(1, NARROW, lambda d: table_copy(d).wait_recv())
        merged = jnp.max(table_in[...], axis=0)
        for o in range(WIDE):
            group = merged[:, o // 4 * 128 : o // 4 * 128 + 128]
            final[o] = pltpu.roll(group, (128 - 32 * (o % 4)) % 128, 1) if o % 4 else group
        final_in[w] = final[w]
        loop(0, WIDE - 1, lambda i: final_copy(peer_step(i)).start())

    def merge_wide():
        loop(0, WIDE - 1, lambda i: final_copy(peer_step(i)).wait_recv())
        best_ref[...] = jnp.max(final_in[...], axis=0)

    for load in loads:
        load.wait()
    tower(0)
    pl.semaphore_wait(barrier, NARROW - 1 + WIDE - 1)
    loop(1, NARROW, lambda d: ids_copy(d).start())
    send_rows(0)
    loop(0, WIDE - 1, lambda i: q_wide_copy(peer_step(i)).start())
    tower(1)
    send_rows(1)
    place_rows()
    pack(0)
    tower(2)
    send_rows(2)
    spread_queries()
    tower(3)
    send_rows(3)
    pack(1)
    local_best()
    pack(2)
    merge_narrow()
    pack(3)
    merge_wide()

    def settle_wide(i):
        k = peer_step(i)
        q_wide_copy(k).wait_send()
        final_copy(k).wait_send()

    def settle_narrow(d):
        ids_copy(d).wait_send()
        q_narrow_copy(d).wait_send()
        table_copy(d).wait_send()

    loop(0, WIDE - 1, settle_wide)
    loop(1, NARROW, settle_narrow)

    for c in range(CHUNKS):
        loop(1, NARROW, lambda d: emb_copy(c, d).wait_send())

    for g in range(GROUPS):

        def settle_group(i):
            data_copy(g, peer_step(i)).wait()
            tag_copy(g, peer_step(i)).wait()

        loop(0, WIDE - 1, settle_group)
        own_data(g).wait()
        own_tag(g).wait()


def run_exchange(features, w_first, w_second, w_third, gain, ids, slots, queries):
    vmem = pl.BlockSpec(memory_space=pltpu.VMEM)
    anywhere = pl.BlockSpec(memory_space=pl.ANY)
    dma = pltpu.SemaphoreType.DMA
    return pl.pallas_call(
        exchange,
        out_shape=(
            jax.ShapeDtypeStruct((WIDE, TOTAL, PIECE), BF16),
            jax.ShapeDtypeStruct((WIDE, GROUPS, 2, 128), F32),
            jax.ShapeDtypeStruct((8, 128), F32),
        ),
        in_specs=[anywhere] * 4 + [vmem] * 4,
        out_specs=(anywhere, anywhere, vmem),
        scratch_shapes=[
            pltpu.VMEM((ROWS, 1024), BF16),
            pltpu.VMEM((1024, 1024), BF16),
            pltpu.VMEM((1024, 1024), BF16),
            pltpu.VMEM((1024, 1024), BF16),
            pltpu.VMEM((NARROW, ROWS, PIECE), BF16),
            pltpu.VMEM((NARROW * ROWS, 256), BF16),
            pltpu.VMEM((WIDE, TOTAL, PIECE), BF16),
            pltpu.VMEM((WIDE, GROUPS, 2, 128), F32),
            pltpu.VMEM((NARROW, 8, 128), jnp.int32),
            pltpu.VMEM((SLOTS, 128), jnp.int32),
            pltpu.VMEM((SLOTS, 128), F32),
            pltpu.VMEM((128, 128), F32),
            pltpu.VMEM((BLOCKS, WIDE, 128), F32),
            pltpu.VMEM((BLOCKS, WIDE, 128), F32),
            pltpu.VMEM((CHUNKS, WIDE, 128), F32),
            pltpu.VMEM((8, 128), F32),
            pltpu.VMEM((WIDE, CAPS[CHUNKS], 256), F32),
            pltpu.VMEM((WIDE, 8, PIECE), F32),
            pltpu.VMEM((4 * WIDE, PIECE), BF16),
            pltpu.VMEM((NARROW, 4 * WIDE, PIECE), BF16),
            pltpu.VMEM((ROWS, ROWS), BF16),
            pltpu.VMEM((SLOTS, ROWS), BF16),
            pltpu.VMEM((NARROW, 8, SLOTS), F32),
            pltpu.VMEM((NARROW, 8, SLOTS), F32),
            pltpu.VMEM((WIDE, 8, 128), F32),
            pltpu.VMEM((WIDE, 8, 128), F32),
            dma((4,)),
            dma((NARROW,)), dma((NARROW,)),
            dma((WIDE,)), dma((WIDE,)),
            dma((NARROW,)), dma((NARROW,)),
            dma((CHUNKS, NARROW)), dma((CHUNKS, NARROW)),
            dma((GROUPS, WIDE)), dma((GROUPS, WIDE)),
            dma((GROUPS, WIDE)), dma((GROUPS, WIDE)),
            dma((NARROW,)), dma((NARROW,)),
            dma((WIDE,)), dma((WIDE,)),
            dma((GROUPS,)), dma((GROUPS,)),
        ],
        compiler_params=pltpu.CompilerParams(
            collective_id=0, has_side_effects=True, vmem_limit_bytes=56 * 2**20
        ),
        name="exchange",
    )(features, w_first, w_second, w_third, gain, ids, slots, queries)


def unpack(arrived_ref, tags_ref, slab_ref):
    spot = iota((CL_DEV * MOST, 1), 0).astype(F32) + 1.0
    parts = []
    for g in range(GROUPS):
        for half in range(2):
            size = min(CAPS[g] - 128 * half, 128)
            if size > 0:
                parts.append(tags_ref[0, g, half : half + 1, :size])
    row = jnp.concatenate(parts, axis=1)
    onehot = jnp.where(spot == row, 1.0, 0.0).astype(BF16)
    slab_ref[0] = jnp.dot(onehot, arrived_ref[0], preferred_element_type=F32).astype(BF16)


def run_unpack(arrived, tags):
    return pl.pallas_call(
        unpack,
        grid=(WIDE,),
        out_shape=jax.ShapeDtypeStruct((WIDE, CL_DEV * MOST, PIECE), BF16),
        in_specs=[
            pl.BlockSpec((1, TOTAL, PIECE), lambda b: (b, 0, 0)),
            pl.BlockSpec((1, GROUPS, 2, 128), lambda b: (b, 0, 0, 0)),
        ],
        out_specs=pl.BlockSpec((1, CL_DEV * MOST, PIECE), lambda b: (b, 0, 0)),
        compiler_params=pltpu.CompilerParams(vmem_limit_bytes=32 * 2**20),
        name="unpack",
    )(arrived, tags)


def pass_on(in_ref, out_ref):
    out_ref[...] = in_ref[...]


def run_pass_on(slab):
    block = pl.BlockSpec((1, CL_DEV * MOST, PIECE), lambda b: (b, 0, 0))
    return pl.pallas_call(
        pass_on,
        grid=(WIDE,),
        out_shape=jax.ShapeDtypeStruct(slab.shape, slab.dtype),
        in_specs=[block],
        out_specs=block,
        name="pass_on",
    )(slab)


def slot_table(id_list, cluster_slots, total):
    levels = jnp.arange(total, dtype=jnp.int32)
    onehot = (id_list[:, None] == levels[None, :]).astype(jnp.bfloat16)
    high_part = (cluster_slots // 64).astype(jnp.bfloat16)
    low_part = (cluster_slots % 64).astype(jnp.bfloat16)
    slot_value = 64.0 * jnp.dot(onehot, high_part, preferred_element_type=jnp.float32) + jnp.dot(
        onehot, low_part, preferred_element_type=jnp.float32
    )
    return (onehot, slot_value.astype(jnp.int32))


def cluster_ranks(onehot):
    count, total = onehot.shape
    block = math.gcd(count, 256)
    number = count // block
    stacked = onehot.reshape(number, block, total)
    inner = jnp.arange(block, dtype=jnp.int32)
    lower = (inner[:, None] >= inner[None, :]).astype(jnp.bfloat16)
    inside = jnp.einsum("rs,bsc->brc", lower, stacked, preferred_element_type=jnp.float32)
    block_sums = inside[:, -1, :]
    outer = jnp.arange(number, dtype=jnp.int32)
    before = (outer[:, None] > outer[None, :]).astype(jnp.float32)
    earlier = jnp.dot(
        before, block_sums, precision=lax.Precision.HIGHEST, preferred_element_type=jnp.float32
    )
    position = jnp.sum(stacked * (inside - 1.0 + earlier[:, None, :]), axis=2)
    return (position.reshape(count).astype(jnp.int32), jnp.sum(block_sums, axis=0))


def padded_slab(features, cluster_ids, cluster_slots, w_first, w_second, w_third, emb_gain):
    first = jax.nn.silu(jnp.dot(features, w_first, preferred_element_type=F32)).astype(BF16)
    second = jax.nn.silu(jnp.dot(first, w_second, preferred_element_type=F32)).astype(BF16)
    raw = jnp.dot(second, w_third, preferred_element_type=F32)
    scale = lax.rsqrt(jnp.mean(raw * raw, axis=1, keepdims=True) + 1e-06)
    embedding = (raw * scale * emb_gain).astype(BF16)
    block_ids = lax.all_gather(cluster_ids[:, 0], "narrow", axis=0, tiled=True)
    block_rows = block_ids.shape[0]
    onehot, slot_of = slot_table(block_ids, cluster_slots, SLOTS)
    positions, _ = cluster_ranks(onehot)
    flat_slot = slot_of * MOST + positions
    sliced = lax.all_to_all(embedding, "narrow", split_axis=1, concat_axis=0, tiled=True)
    source = (
        jnp.full((SLOTS * MOST,), block_rows, jnp.int32)
        .at[flat_slot]
        .set(jnp.arange(block_rows, dtype=jnp.int32))
    )
    padded = jnp.concatenate([sliced, jnp.zeros((1, PIECE), BF16)], axis=0)
    outgoing = jnp.take(padded, source, axis=0).reshape(WIDE, CL_DEV * MOST, PIECE)
    return run_pass_on(lax.all_to_all(outgoing, "wide", split_axis=0, concat_axis=0, tiled=True))


def shards(features, cluster_ids, cluster_slots, w_first, w_second, w_third, emb_gain, queries):
    ids = cluster_ids.reshape(8, 128)
    query = jnp.pad(queries.astype(F32), ((0, 4), (0, 0)))
    arrived, tags, best = run_exchange(
        features, w_first, w_second, w_third, emb_gain.reshape(1, 1024), ids, cluster_slots.reshape(1, SLOTS), query
    )
    fits = jnp.max(tags[:, CHUNKS, 1, 0]) == 0.0
    slab = lax.cond(
        fits,
        lambda: run_unpack(arrived, tags),
        lambda: padded_slab(features, cluster_ids, cluster_slots, w_first, w_second, w_third, emb_gain),
    )
    return (best[:, :CL_DEV], slab.reshape(WIDE, CL_DEV, MOST, PIECE))


def solution(mesh):
    placed = (
        P(("wide", "narrow"), None),
        P(("wide", "narrow"), None),
        P(),
        P(),
        P(),
        P(),
        P(),
        P("wide", "narrow"),
    )
    return jax.shard_map(
        shards,
        mesh=mesh,
        in_specs=placed,
        out_specs=(P("narrow", "wide"), P(None, "wide", None, "narrow")),
        check_vma=False,
    )
```

```python
import functools
import math

import jax
import jax.numpy as jnp
from jax import lax
from jax.experimental import pallas as pl
from jax.experimental.pallas import tpu as pltpu
from jax.sharding import PartitionSpec as P

MESH = pl.DeviceIdType.MESH
CL_DEV = 32
MOST = 32
WIDE = 16
NARROW = 8
ROWS = 1024
PIECE = 128
SLOTS = 512
CHUNKS = 4
CHUNK = ROWS // CHUNKS
PARTS = CHUNK // 128
CAP = 176
OVER = 48
GROUPS = CHUNKS + 1
TOTAL = CHUNKS * CAP + OVER
BLOCKS = NARROW * ROWS // 128
SELF = 2
BATCH = 4
NT = (((1,), (1,)), ((), ()))
F32 = jnp.float32
BF16 = jnp.bfloat16


def silu(v):
    half = 0.5 * v
    return half + half * jnp.tanh(half)


def loop(low, high, body):
    def step(i, carry):
        body(i)
        return carry

    lax.fori_loop(low, high, step, 0)


def peer_step(i):
    return i + (i + 13) // 15


def iota(shape, dim):
    return lax.broadcasted_iota(jnp.int32, shape, dim)


def exchange(
    feats_hbm, w1_hbm, w2_hbm, w3_hbm, gain_ref, ids_ref, slots_ref, query_ref,
    arrived_ref, tags_ref, best_ref,
    feats, w1, w2, w3, emb, rhs, stage, tag_out, notes, notes_all, rank_all, owner_of, levels, dest, dest_over, spill, over_sum,
    q_wide, q_mine, q_all, perm, ends, table, table_in, final, final_in,
    load_sem, notes_s, notes_r, qw_s, qw_r, qn_s, qn_r, emb_s, emb_r, data_s, data_r, tag_s, tag_r,
    table_s, table_r, final_s, final_r, own_sem, own_tag_sem,
):
    w = lax.axis_index("wide")
    n = lax.axis_index("narrow")

    def wide_peer(k):
        down = (2 + k) % 4
        across = (2 + k + k // 4) % 4
        return ((w // 4 + down) % 4) * 4 + (w % 4 + across) % 4

    def narrow_peer(d):
        return (n + d) % NARROW

    def remote(src, dst, send, recv, device):
        return pltpu.make_async_remote_copy(
            src_ref=src, dst_ref=dst, send_sem=send, recv_sem=recv, device_id=device, device_id_type=MESH
        )

    def notes_copy(d):
        return remote(notes, notes_all.at[n], notes_s.at[d], notes_r.at[d], (w, narrow_peer(d)))

    def q_wide_copy(k):
        return remote(query_ref, q_wide.at[w], qw_s.at[k], qw_r.at[k], (wide_peer(k), n))

    def q_narrow_copy(d):
        return remote(q_mine, q_all.at[n], qn_s.at[d], qn_r.at[d], (w, narrow_peer(d)))

    def rows_of(c):
        return pl.ds(pl.multiple_of(c * CHUNK, CHUNK), CHUNK)

    def landing(c, m):
        return pl.ds(pl.multiple_of((NARROW * c + m) * CHUNK, CHUNK), CHUNK)

    def emb_copy(c, d):
        to = narrow_peer(d)
        return remote(
            emb.at[to, rows_of(c)], rhs.at[landing(c, n), pl.ds(0, 128)],
            emb_s.at[c, d], emb_r.at[c, d], (w, to),
        )

    def packed_rows(g, last=False):
        return pl.ds(pl.multiple_of(g * CAP, 16), OVER if last else CAP)

    def data_copy(g, k, last=False):
        rows = packed_rows(g, last)
        return remote(
            stage.at[k, rows], arrived_ref.at[w, rows],
            data_s.at[g, k], data_r.at[g, k], (wide_peer(k), n),
        )

    def tag_copy(g, k):
        return remote(tag_out.at[k, g], tags_ref.at[w, g], tag_s.at[g, k], tag_r.at[g, k], (wide_peer(k), n))

    def table_copy(d):
        to = narrow_peer(d)
        return remote(table.at[to], table_in.at[n], table_s.at[d], table_r.at[d], (w, to))

    def final_copy(k):
        to = wide_peer(k)
        return remote(final.at[to], final_in.at[w], final_s.at[k], final_r.at[k], (to, n))

    def own_data(g, last=False):
        rows = packed_rows(g, last)
        return pltpu.make_async_copy(stage.at[SELF, rows], arrived_ref.at[w, rows], own_sem.at[g])

    def own_tag(g):
        return pltpu.make_async_copy(tag_out.at[SELF, g], tags_ref.at[w, g], own_tag_sem.at[g])

    def load(src, dst, part, i):
        rows = pl.ds(part * 256, 256)
        return pltpu.make_async_copy(src.at[rows], dst.at[rows], load_sem.at[i, part])

    feat_loads = [load(feats_hbm, feats, part, 0) for part in range(4)]
    weight_loads = [
        [load(src, dst, part, i + 1) for part in range(4)]
        for i, (src, dst) in enumerate(((w1_hbm, w1), (w2_hbm, w2), (w3_hbm, w3)))
    ]
    feat_loads[0].start()
    for group in weight_loads:
        for copy in group:
            copy.start()
    for copy in feat_loads[1:]:
        copy.start()

    barrier = pltpu.get_barrier_semaphore()

    def greet_wide(i):
        pl.semaphore_signal(barrier, inc=1, device_id=(wide_peer(peer_step(i)), n), device_id_type=MESH)

    def greet_narrow(d):
        pl.semaphore_signal(barrier, inc=1, device_id=(w, narrow_peer(d)), device_id_type=MESH)

    loop(1, NARROW, greet_narrow)
    loop(0, WIDE - 1, greet_wide)

    slot_level = iota((SLOTS, SLOTS), 0)
    cluster_level = iota((SLOTS, SLOTS), 1).astype(F32)
    holder = jnp.sum(jnp.where(slots_ref[...] == slot_level, cluster_level, 0.0), axis=1, keepdims=True)
    owner_of[...] = jnp.broadcast_to(holder, (SLOTS, 128)).astype(jnp.int32)
    q_wide[w] = query_ref[...]
    sums = (iota((128, 256), 0) <= iota((128, 256), 1)).astype(F32).astype(BF16)

    def note_rows():
        slot = iota((SLOTS, 128), 0)
        place = (slot % CL_DEV * MOST).astype(F32)
        level = slot.astype(F32)
        levels[...] = place

        def note(k):
            lanes = pl.ds(pl.multiple_of(k * 128, 128), 128)
            named = owner_of[...] == ids_ref[pl.ds(k, 1), :]
            onehot = jnp.where(named, 1.0, 0.0).astype(BF16)
            ends[:, lanes] = onehot
            counts = jnp.dot(onehot, sums, preferred_element_type=F32)
            spot = jnp.where(named, counts[:, :128] + levels[...], 0.0)
            notes[pl.ds(8 + k, 1), :] = jnp.sum(spot, axis=0, keepdims=True)
            notes[pl.ds(k, 1), :] = jnp.sum(jnp.where(named, level, 0.0), axis=0, keepdims=True)
            levels[...] += counts[:, 128:]

        loop(0, 8, note)
        number = (levels[...] - place).reshape(WIDE, CL_DEV, 128)
        inner = (iota((CL_DEV, 128), 0) == iota((CL_DEV, 128), 1)).astype(F32)
        notes[16:32, :] = jnp.sum(number * inner[None], axis=1)
        notes_all[n] = notes[...]

    def tower(c):
        x = feats[rows_of(c), :]
        first = silu(jnp.dot(x, w1[...], preferred_element_type=F32)).astype(BF16)
        second = silu(jnp.dot(first, w2[...], preferred_element_type=F32)).astype(BF16)
        raw = jnp.dot(second, w3[...], preferred_element_type=F32)
        scale = lax.rsqrt(jnp.mean(raw * raw, axis=1, keepdims=True) + 1e-06)
        embedding = (raw * scale * gain_ref[...]).astype(BF16)
        for j in range(NARROW):
            emb[j, rows_of(c), :] = embedding[:, j * PIECE : (j + 1) * PIECE]
        rhs[landing(c, n), 0:128] = emb[n, rows_of(c), :]

    def send_rows(c):
        loop(1, NARROW, lambda d: emb_copy(c, d).start())

    def place_rows():
        loop(1, NARROW, lambda d: notes_copy(d).wait_recv())
        earlier = [jnp.zeros((WIDE, 128), F32)]
        for m in range(NARROW - 1):
            earlier.append(earlier[m] + notes_all[m, 16:32, :])
        earlier = [number.astype(BF16) for number in earlier]
        inside_level = iota((128, 128), 0).astype(F32)
        owner_level = iota((WIDE, 128), 0).astype(F32)
        cap = float(CAP)

        def place_chunk(c, before):
            held = []
            for m in range(NARROW):
                for part in range(PARTS):
                    k = PARTS * c + part
                    row = notes_all[m, pl.ds(k, 1), :]
                    owner = jnp.floor(row * (1.0 / CL_DEV))
                    held.append(jnp.where(owner_level == owner, 1.0, 0.0))
                    inside = jnp.where(inside_level == row - owner * CL_DEV, 1.0, 0.0).astype(BF16)
                    ahead = jnp.dot(earlier[m], inside, preferred_element_type=F32) * held[-1]
                    rank_all[m, pl.ds(k, 1), :] = notes_all[m, pl.ds(8 + k, 1), :] + jnp.sum(
                        ahead, axis=0, keepdims=True
                    )
            ordered = jnp.dot(jnp.concatenate(held, axis=0).astype(BF16), sums, preferred_element_type=F32)
            carry = jnp.zeros((WIDE, 128), F32)
            for q in range(NARROW * PARTS):
                spot = ordered[WIDE * q : WIDE * (q + 1), :128] + carry - 1.0
                spot = jnp.where(held[q] > 0.0, spot, -1.0)
                dest[NARROW * PARTS * c + q] = spot
                dest_over[NARROW * PARTS * c + q] = jnp.where(spot >= cap, spot - cap + before, -1.0)
                carry = carry + ordered[WIDE * q : WIDE * (q + 1), 128:]
            return before + jnp.maximum(carry - cap, 0.0)

        before = lax.fori_loop(0, CHUNKS, place_chunk, jnp.zeros((WIDE, 128), F32))
        most = jnp.max(before, axis=0, keepdims=True)
        spill[...] = jnp.broadcast_to(jnp.where(most > float(OVER), 1.0, 0.0), spill.shape)

        ranks = rank_all[...].reshape(BLOCKS, 128)
        turned = jnp.transpose(jnp.concatenate([ranks, jnp.zeros((128 - BLOCKS, 128), F32)], axis=0))
        left = iota((128, 128), 1) < 64

        def tag_chunk(c):
            moved = pltpu.roll(turned, (128 - PARTS * c) % 128, 1)
            for m in range(NARROW):
                for part in range(PARTS):
                    at = 8 * m + part
                    column = jnp.broadcast_to(moved[:, at : at + 1], (128, 128))
                    high = jnp.floor(column * (1.0 / 32.0)) * 32.0
                    rows = pl.ds(pl.multiple_of((NARROW * c + m) * CHUNK + part * 128, 128), 128)
                    rhs[rows, 128:256] = jnp.where(left, high, column - high).astype(BF16)

        loop(0, CHUNKS, tag_chunk)

    def spread_queries():
        loop(0, WIDE - 1, lambda i: q_wide_copy(peer_step(i)).wait_recv())
        at = iota((4 * WIDE, 8 * WIDE), 0)
        pick = iota((4 * WIDE, 8 * WIDE), 1) == at // 4 * 8 + at % 4
        spread = q_wide[...].reshape(8 * WIDE, PIECE).astype(BF16)
        q_mine[...] = jnp.dot(pick.astype(F32).astype(BF16), spread, preferred_element_type=F32).astype(BF16)
        q_all[n] = q_mine[...]
        loop(1, NARROW, lambda d: q_narrow_copy(d).start())

    def write_tag(k, g, tag, cap):
        tag = tag + pltpu.roll(tag, 64, 1)
        for half in range(2):
            size = min(cap - 128 * half, 128)
            if size > 0:
                eye = iota((size, 128), 0) == iota((size, 128), 1)
                line = jnp.sum(jnp.where(eye, tag[128 * half : 128 * half + size], 0.0), axis=0, keepdims=True)
            else:
                line = spill[0:1, :]
            tag_out[k, g, half : half + 1, :] = line

    def send_group(k, g, last=False):
        @pl.when(k != SELF)
        def _():
            data_copy(g, k, last).start()
            tag_copy(g, k).start()

        @pl.when(k == SELF)
        def _():
            own_data(g, last).start()
            own_tag(g).start()

    def pack(c):
        loop(1, NARROW, lambda d: emb_copy(c, d).wait_recv())
        blocks = NARROW * PARTS
        both = CAP + OVER
        spot = iota((CAP, 128), 0).astype(F32)
        spot_over = iota((OVER, 128), 0).astype(F32)

        def to_owners(i):
            lines = []
            for j in range(BATCH):
                to = wide_peer(BATCH * i + j)
                for spots, level in ((dest, spot), (dest_over, spot_over)):
                    parts = []
                    for q in range(blocks):
                        row = spots[blocks * c + q, pl.ds(to, 1), :]
                        parts.append(jnp.where(level == row, 1.0, 0.0).astype(BF16))
                    lines.append(jnp.concatenate(parts, axis=1))
            onehot = jnp.concatenate(lines, axis=0)
            source = rhs[pl.ds(pl.multiple_of(c * (NARROW * CHUNK), NARROW * CHUNK), NARROW * CHUNK), :]
            packed = jnp.dot(onehot, source, preferred_element_type=F32)
            for j in range(BATCH):
                k = BATCH * i + j
                main = packed[both * j : both * j + CAP]
                stage[k, packed_rows(c), :] = main[:, :128].astype(BF16)
                write_tag(k, c, main[:, 128:], CAP)
                send_group(k, c)
                over_sum[k] += packed[both * j + CAP : both * (j + 1)]

        loop(0, WIDE // BATCH, to_owners)

    def pack_over():
        def to_owner(k):
            rest = over_sum[k]
            stage[k, packed_rows(CHUNKS, True), :] = rest[:, :128].astype(BF16)
            write_tag(k, CHUNKS, rest[:, 128:], OVER)
            send_group(k, CHUNKS, True)

        loop(0, WIDE, to_owner)

    def local_best():
        loop(1, NARROW, lambda d: q_narrow_copy(d).wait_recv())
        score = jnp.zeros((4 * WIDE, ROWS), F32)
        for j in range(NARROW):
            score += lax.dot_general(q_all[j], emb[j], NT, preferred_element_type=F32)
        ids_f = ids_ref[...].astype(F32)
        id_row = jnp.concatenate([ids_f[k : k + 1, :] for k in range(8)], axis=1)
        key_row = id_row * float(ROWS) + iota((1, ROWS), 1).astype(F32)
        eye = iota((128, 128), 0) == iota((128, 128), 1)
        order = iota((128, ROWS), 1).astype(F32)
        for k in range(8):
            key = jnp.sum(jnp.where(eye, key_row[:, k * 128 : (k + 1) * 128], 0.0), axis=1, keepdims=True)
            position = jnp.sum(jnp.where(key_row < key, 1.0, 0.0), axis=1, keepdims=True)
            perm[k * 128 : (k + 1) * 128, :] = jnp.where(order == position, 1.0, 0.0).astype(BF16)
        high = score.astype(BF16)
        low = (score - high.astype(F32)).astype(BF16)
        id_high = jnp.floor(id_row * (1.0 / 32.0)) * 32.0
        line = iota((16, ROWS), 0)
        extra = jnp.where(line == 0, id_high, jnp.where(line == 1, id_row - id_high, 0.0)).astype(BF16)
        arranged = jnp.dot(jnp.concatenate([high, low, extra], axis=0), perm[...], preferred_element_type=F32)
        top = arranged[0:64] + arranged[64:128]
        seg = jnp.broadcast_to(arranged[128:129] + arranged[129:130], (8, ROWS))
        lane = iota((8, ROWS), 1)
        for step in (1, 2, 4, 8, 16):
            same = (pltpu.roll(seg, step, 1) == seg) & (lane >= step)
            gate = jnp.where(same, 0.0, -jnp.inf)[0:1]
            top = jnp.maximum(top, pltpu.roll(top, step, 1) + gate)
        closing = (pltpu.roll(seg, ROWS - 1, 1) != seg) | (lane == ROWS - 1)
        end_id = jnp.where(closing, seg, -1.0)[0:1]
        for k in range(ROWS // 128):
            match = owner_of[...].astype(F32) == end_id[:, k * 128 : (k + 1) * 128]
            ends[:, k * 128 : (k + 1) * 128] = jnp.where(match, 1.0, 0.0).astype(BF16)
        high = top.astype(BF16)
        low = (top - high.astype(F32)).astype(BF16)
        ones = jnp.ones((16, ROWS), BF16)
        found = lax.dot_general(jnp.concatenate([high, low, ones], axis=0), ends[...], NT, preferred_element_type=F32)
        by_slot = jnp.where(found[128:129] > 0.0, found[0:64] + found[64:128], -jnp.inf)
        for j in range(NARROW):
            table[j] = by_slot[8 * j : 8 * j + 8]
        table_in[n] = table[n]
        loop(1, NARROW, lambda d: table_copy(d).start())

    def merge_narrow():
        loop(1, NARROW, lambda d: table_copy(d).wait_recv())
        merged = jnp.max(table_in[...], axis=0)
        for o in range(WIDE):
            group = merged[:, o // 4 * 128 : o // 4 * 128 + 128]
            final[o] = pltpu.roll(group, (128 - 32 * (o % 4)) % 128, 1) if o % 4 else group
        final_in[w] = final[w]
        loop(0, WIDE - 1, lambda i: final_copy(peer_step(i)).start())

    def merge_wide():
        loop(0, WIDE - 1, lambda i: final_copy(peer_step(i)).wait_recv())
        best_ref[...] = jnp.max(final_in[...], axis=0)

    over_sum[...] = jnp.zeros_like(over_sum)
    note_rows()
    for group in [feat_loads] + weight_loads:
        for copy in group:
            copy.wait()

    def turn(t):
        @pl.when(t < CHUNKS)
        def _():
            tower(t)

        @pl.when(t == 0)
        def _():
            pl.semaphore_wait(barrier, NARROW - 1 + WIDE - 1)
            loop(1, NARROW, lambda d: notes_copy(d).start())

        @pl.when(t < CHUNKS)
        def _():
            send_rows(t)

        @pl.when(t == 0)
        def _():
            loop(0, WIDE - 1, lambda i: q_wide_copy(peer_step(i)).start())

        @pl.when(t == 1)
        def _():
            place_rows()

        @pl.when(t == 2)
        def _():
            spread_queries()

        @pl.when(t == CHUNKS)
        def _():
            local_best()

        @pl.when(t >= 1)
        def _():
            pack(t - 1)

    loop(0, CHUNKS + 1, turn)
    pack_over()
    merge_narrow()
    merge_wide()

    def settle_wide(i):
        k = peer_step(i)
        q_wide_copy(k).wait_send()
        final_copy(k).wait_send()

    def settle_narrow(d):
        notes_copy(d).wait_send()
        q_narrow_copy(d).wait_send()
        table_copy(d).wait_send()

    loop(0, WIDE - 1, settle_wide)
    loop(1, NARROW, settle_narrow)

    def settle_chunk(c):
        loop(1, NARROW, lambda d: emb_copy(c, d).wait_send())
        settle_group(c, False)

    def settle_group(g, last):
        def settle(i):
            data_copy(g, peer_step(i), last).wait()
            tag_copy(g, peer_step(i)).wait()

        loop(0, WIDE - 1, settle)
        own_data(g, last).wait()
        own_tag(g).wait()

    loop(0, CHUNKS, settle_chunk)
    settle_group(CHUNKS, True)


def run_exchange(features, w_first, w_second, w_third, gain, ids, slots, queries):
    vmem = pl.BlockSpec(memory_space=pltpu.VMEM)
    anywhere = pl.BlockSpec(memory_space=pl.ANY)
    dma = pltpu.SemaphoreType.DMA
    return pl.pallas_call(
        exchange,
        out_shape=(
            jax.ShapeDtypeStruct((WIDE, TOTAL, PIECE), BF16),
            jax.ShapeDtypeStruct((WIDE, GROUPS, 2, 128), F32),
            jax.ShapeDtypeStruct((8, 128), F32),
        ),
        in_specs=[anywhere] * 4 + [vmem] * 4,
        out_specs=(anywhere, anywhere, vmem),
        scratch_shapes=[
            pltpu.VMEM((ROWS, 1024), BF16),
            pltpu.VMEM((1024, 1024), BF16),
            pltpu.VMEM((1024, 1024), BF16),
            pltpu.VMEM((1024, 1024), BF16),
            pltpu.VMEM((NARROW, ROWS, PIECE), BF16),
            pltpu.VMEM((NARROW * ROWS, 256), BF16),
            pltpu.VMEM((WIDE, TOTAL, PIECE), BF16),
            pltpu.VMEM((WIDE, GROUPS, 2, 128), F32),
            pltpu.VMEM((32, 128), F32),
            pltpu.VMEM((NARROW, 32, 128), F32),
            pltpu.VMEM((NARROW, 8, 128), F32),
            pltpu.VMEM((SLOTS, 128), jnp.int32),
            pltpu.VMEM((SLOTS, 128), F32),
            pltpu.VMEM((BLOCKS, WIDE, 128), F32),
            pltpu.VMEM((BLOCKS, WIDE, 128), F32),
            pltpu.VMEM((8, 128), F32),
            pltpu.VMEM((WIDE, OVER, 256), F32),
            pltpu.VMEM((WIDE, 8, PIECE), F32),
            pltpu.VMEM((4 * WIDE, PIECE), BF16),
            pltpu.VMEM((NARROW, 4 * WIDE, PIECE), BF16),
            pltpu.VMEM((ROWS, ROWS), BF16),
            pltpu.VMEM((SLOTS, ROWS), BF16),
            pltpu.VMEM((NARROW, 8, SLOTS), F32),
            pltpu.VMEM((NARROW, 8, SLOTS), F32),
            pltpu.VMEM((WIDE, 8, 128), F32),
            pltpu.VMEM((WIDE, 8, 128), F32),
            dma((4, 4)),
            dma((NARROW,)), dma((NARROW,)),
            dma((WIDE,)), dma((WIDE,)),
            dma((NARROW,)), dma((NARROW,)),
            dma((CHUNKS, NARROW)), dma((CHUNKS, NARROW)),
            dma((GROUPS, WIDE)), dma((GROUPS, WIDE)),
            dma((GROUPS, WIDE)), dma((GROUPS, WIDE)),
            dma((NARROW,)), dma((NARROW,)),
            dma((WIDE,)), dma((WIDE,)),
            dma((GROUPS,)), dma((GROUPS,)),
        ],
        compiler_params=pltpu.CompilerParams(
            collective_id=0, has_side_effects=True, vmem_limit_bytes=56 * 2**20
        ),
        name="exchange",
    )(features, w_first, w_second, w_third, gain, ids, slots, queries)


def unpack(arrived_ref, tags_ref, slab_ref):
    spot = iota((CL_DEV * MOST, 1), 0).astype(F32) + 1.0
    parts = []
    for g in range(GROUPS):
        for half in range(2):
            size = min((CAP if g < CHUNKS else OVER) - 128 * half, 128)
            if size > 0:
                parts.append(tags_ref[0, g, half : half + 1, :size])
    row = jnp.concatenate(parts, axis=1)
    onehot = jnp.where(spot == row, 1.0, 0.0).astype(BF16)
    slab_ref[0] = jnp.dot(onehot, arrived_ref[0], preferred_element_type=F32).astype(BF16)


def run_unpack(arrived, tags):
    return pl.pallas_call(
        unpack,
        grid=(WIDE,),
        out_shape=jax.ShapeDtypeStruct((WIDE, CL_DEV * MOST, PIECE), BF16),
        in_specs=[
            pl.BlockSpec((1, TOTAL, PIECE), lambda b: (b, 0, 0)),
            pl.BlockSpec((1, GROUPS, 2, 128), lambda b: (b, 0, 0, 0)),
        ],
        out_specs=pl.BlockSpec((1, CL_DEV * MOST, PIECE), lambda b: (b, 0, 0)),
        compiler_params=pltpu.CompilerParams(vmem_limit_bytes=32 * 2**20),
        name="unpack",
    )(arrived, tags)


def pass_on(in_ref, out_ref):
    out_ref[...] = in_ref[...]


def run_pass_on(slab):
    block = pl.BlockSpec((1, CL_DEV * MOST, PIECE), lambda b: (b, 0, 0))
    return pl.pallas_call(
        pass_on,
        grid=(WIDE,),
        out_shape=jax.ShapeDtypeStruct(slab.shape, slab.dtype),
        in_specs=[block],
        out_specs=block,
        name="pass_on",
    )(slab)


def slot_table(id_list, cluster_slots, total):
    levels = jnp.arange(total, dtype=jnp.int32)
    onehot = (id_list[:, None] == levels[None, :]).astype(jnp.bfloat16)
    high_part = (cluster_slots // 64).astype(jnp.bfloat16)
    low_part = (cluster_slots % 64).astype(jnp.bfloat16)
    slot_value = 64.0 * jnp.dot(onehot, high_part, preferred_element_type=jnp.float32) + jnp.dot(
        onehot, low_part, preferred_element_type=jnp.float32
    )
    return (onehot, slot_value.astype(jnp.int32))


def cluster_ranks(onehot):
    count, total = onehot.shape
    block = math.gcd(count, 256)
    number = count // block
    stacked = onehot.reshape(number, block, total)
    inner = jnp.arange(block, dtype=jnp.int32)
    lower = (inner[:, None] >= inner[None, :]).astype(jnp.bfloat16)
    inside = jnp.einsum("rs,bsc->brc", lower, stacked, preferred_element_type=jnp.float32)
    block_sums = inside[:, -1, :]
    outer = jnp.arange(number, dtype=jnp.int32)
    before = (outer[:, None] > outer[None, :]).astype(jnp.float32)
    earlier = jnp.dot(
        before, block_sums, precision=lax.Precision.HIGHEST, preferred_element_type=jnp.float32
    )
    position = jnp.sum(stacked * (inside - 1.0 + earlier[:, None, :]), axis=2)
    return (position.reshape(count).astype(jnp.int32), jnp.sum(block_sums, axis=0))


def padded_slab(features, cluster_ids, cluster_slots, w_first, w_second, w_third, emb_gain):
    first = jax.nn.silu(jnp.dot(features, w_first, preferred_element_type=F32)).astype(BF16)
    second = jax.nn.silu(jnp.dot(first, w_second, preferred_element_type=F32)).astype(BF16)
    raw = jnp.dot(second, w_third, preferred_element_type=F32)
    scale = lax.rsqrt(jnp.mean(raw * raw, axis=1, keepdims=True) + 1e-06)
    embedding = (raw * scale * emb_gain).astype(BF16)
    block_ids = lax.all_gather(cluster_ids[:, 0], "narrow", axis=0, tiled=True)
    block_rows = block_ids.shape[0]
    onehot, slot_of = slot_table(block_ids, cluster_slots, SLOTS)
    positions, _ = cluster_ranks(onehot)
    flat_slot = slot_of * MOST + positions
    sliced = lax.all_to_all(embedding, "narrow", split_axis=1, concat_axis=0, tiled=True)
    source = (
        jnp.full((SLOTS * MOST,), block_rows, jnp.int32)
        .at[flat_slot]
        .set(jnp.arange(block_rows, dtype=jnp.int32))
    )
    padded = jnp.concatenate([sliced, jnp.zeros((1, PIECE), BF16)], axis=0)
    outgoing = jnp.take(padded, source, axis=0).reshape(WIDE, CL_DEV * MOST, PIECE)
    return run_pass_on(lax.all_to_all(outgoing, "wide", split_axis=0, concat_axis=0, tiled=True))


def shards(features, cluster_ids, cluster_slots, w_first, w_second, w_third, emb_gain, queries):
    ids = cluster_ids.reshape(8, 128)
    query = jnp.pad(queries.astype(F32), ((0, 4), (0, 0)))
    arrived, tags, best = run_exchange(
        features, w_first, w_second, w_third, emb_gain.reshape(1, 1024), ids, cluster_slots.reshape(1, SLOTS), query
    )
    fits = jnp.max(tags[:, CHUNKS, 1, 0]) == 0.0
    slab = lax.cond(
        fits,
        lambda: run_unpack(arrived, tags),
        lambda: padded_slab(features, cluster_ids, cluster_slots, w_first, w_second, w_third, emb_gain),
    )
    return (best[:, :CL_DEV], slab.reshape(WIDE, CL_DEV, MOST, PIECE))


def solution(mesh):
    placed = (
        P(("wide", "narrow"), None),
        P(("wide", "narrow"), None),
        P(),
        P(),
        P(),
        P(),
        P(),
        P("wide", "narrow"),
    )
    return jax.shard_map(
        shards,
        mesh=mesh,
        in_specs=placed,
        out_specs=(P("narrow", "wide"), P(None, "wide", None, "narrow")),
        check_vma=False,
    )
```

```python
import functools
import math

import jax
import jax.numpy as jnp
from jax import lax
from jax.experimental import pallas as pl
from jax.experimental.pallas import tpu as pltpu
from jax.sharding import PartitionSpec as P

MESH = pl.DeviceIdType.MESH
CL_DEV = 32
MOST = 32
WIDE = 16
NARROW = 8
ROWS = 1024
PIECE = 128
SLOTS = 512
CHUNKS = 4
CHUNK = ROWS // CHUNKS
PARTS = CHUNK // 128
CAP = 176
OVER = 48
GROUPS = CHUNKS + 1
TOTAL = CHUNKS * CAP + OVER
BLOCKS = NARROW * ROWS // 128
SELF = 2
BATCH = 4
NT = (((1,), (1,)), ((), ()))
F32 = jnp.float32
BF16 = jnp.bfloat16


def silu(v):
    half = 0.5 * v
    return half + half * jnp.tanh(half)


def loop(low, high, body):
    def step(i, carry):
        body(i)
        return carry

    lax.fori_loop(low, high, step, 0)


def peer_step(i):
    return i + (i + 13) // 15


def iota(shape, dim):
    return lax.broadcasted_iota(jnp.int32, shape, dim)


def exchange(
    feats_hbm, w1_hbm, w2_hbm, w3_hbm, gain_ref, ids_ref, slots_ref, query_ref,
    arrived_ref, tags_ref, best_ref,
    feats, w1, w2, w3, emb, rhs, stage, tag_out, notes, notes_all, rank_all, owner_of, levels, dest, dest_over, spill, over_sum,
    q_wide, q_mine, q_all, perm, ends, table, table_in, final, final_in,
    load_sem, notes_s, notes_r, qw_s, qw_r, qn_s, qn_r, emb_s, emb_r, data_s, data_r, tag_s, tag_r,
    table_s, table_r, final_s, final_r, own_sem, own_tag_sem,
):
    w = lax.axis_index("wide")
    n = lax.axis_index("narrow")

    def wide_peer(k):
        down = (2 + k) % 4
        across = (2 + k + k // 4) % 4
        return ((w // 4 + down) % 4) * 4 + (w % 4 + across) % 4

    def narrow_peer(d):
        return (n + d) % NARROW

    def remote(src, dst, send, recv, device):
        return pltpu.make_async_remote_copy(
            src_ref=src, dst_ref=dst, send_sem=send, recv_sem=recv, device_id=device, device_id_type=MESH
        )

    def notes_copy(d):
        return remote(notes, notes_all.at[n], notes_s.at[d], notes_r.at[d], (w, narrow_peer(d)))

    def q_wide_copy(k):
        return remote(query_ref, q_wide.at[w], qw_s.at[k], qw_r.at[k], (wide_peer(k), n))

    def q_narrow_copy(d):
        return remote(q_mine, q_all.at[n], qn_s.at[d], qn_r.at[d], (w, narrow_peer(d)))

    def rows_of(c):
        return pl.ds(pl.multiple_of(c * CHUNK, CHUNK), CHUNK)

    def landing(c, m):
        return pl.ds(pl.multiple_of((NARROW * c + m) * CHUNK, CHUNK), CHUNK)

    def emb_copy(c, d):
        to = narrow_peer(d)
        return remote(
            emb.at[to, rows_of(c)], rhs.at[landing(c, n), pl.ds(0, 128)],
            emb_s.at[c, d], emb_r.at[c, d], (w, to),
        )

    def packed_rows(g, last=False):
        return pl.ds(pl.multiple_of(g * CAP, 16), OVER if last else CAP)

    def data_copy(g, k, last=False):
        rows = packed_rows(g, last)
        return remote(
            stage.at[k, rows], arrived_ref.at[w, rows],
            data_s.at[g, k], data_r.at[g, k], (wide_peer(k), n),
        )

    def tag_copy(g, k):
        return remote(tag_out.at[k, g], tags_ref.at[w, g], tag_s.at[g, k], tag_r.at[g, k], (wide_peer(k), n))

    def table_copy(d):
        to = narrow_peer(d)
        return remote(table.at[to], table_in.at[n], table_s.at[d], table_r.at[d], (w, to))

    def final_copy(k):
        to = wide_peer(k)
        return remote(final.at[to], final_in.at[w], final_s.at[k], final_r.at[k], (to, n))

    def own_data(g, last=False):
        rows = packed_rows(g, last)
        return pltpu.make_async_copy(stage.at[SELF, rows], arrived_ref.at[w, rows], own_sem.at[g])

    def own_tag(g):
        return pltpu.make_async_copy(tag_out.at[SELF, g], tags_ref.at[w, g], own_tag_sem.at[g])

    def load(src, dst, part, i):
        rows = pl.ds(part * 256, 256)
        return pltpu.make_async_copy(src.at[rows], dst.at[rows], load_sem.at[i, part])

    feat_loads = [load(feats_hbm, feats, part, 0) for part in range(4)]
    weight_loads = [
        [load(src, dst, part, i + 1) for part in range(4)]
        for i, (src, dst) in enumerate(((w1_hbm, w1), (w2_hbm, w2), (w3_hbm, w3)))
    ]
    feat_loads[0].start()
    for group in weight_loads:
        for copy in group:
            copy.start()
    for copy in feat_loads[1:]:
        copy.start()

    barrier = pltpu.get_barrier_semaphore()

    def greet_wide(i):
        pl.semaphore_signal(barrier, inc=1, device_id=(wide_peer(peer_step(i)), n), device_id_type=MESH)

    def greet_narrow(d):
        pl.semaphore_signal(barrier, inc=1, device_id=(w, narrow_peer(d)), device_id_type=MESH)

    loop(1, NARROW, greet_narrow)
    loop(0, WIDE - 1, greet_wide)

    slot_level = iota((SLOTS, SLOTS), 0)
    cluster_level = iota((SLOTS, SLOTS), 1).astype(F32)
    holder = jnp.sum(jnp.where(slots_ref[...] == slot_level, cluster_level, 0.0), axis=1, keepdims=True)
    owner_of[...] = jnp.broadcast_to(holder, (SLOTS, 128)).astype(jnp.int32)
    q_wide[w] = query_ref[...]
    sums = (iota((128, 256), 0) <= iota((128, 256), 1)).astype(F32).astype(BF16)

    def note_rows():
        slot = iota((SLOTS, 128), 0)
        place = (slot % CL_DEV * MOST).astype(F32)
        level = slot.astype(F32)
        levels[...] = place

        def note(k):
            lanes = pl.ds(pl.multiple_of(k * 128, 128), 128)
            named = owner_of[...] == ids_ref[pl.ds(k, 1), :]
            onehot = jnp.where(named, 1.0, 0.0).astype(BF16)
            ends[:, lanes] = onehot
            counts = jnp.dot(onehot, sums, preferred_element_type=F32)
            spot = jnp.where(named, counts[:, :128] + levels[...], 0.0)
            notes[pl.ds(8 + k, 1), :] = jnp.sum(spot, axis=0, keepdims=True)
            notes[pl.ds(k, 1), :] = jnp.sum(jnp.where(named, level, 0.0), axis=0, keepdims=True)
            levels[...] += counts[:, 128:]

        loop(0, 8, note)
        number = (levels[...] - place).reshape(WIDE, CL_DEV, 128)
        inner = (iota((CL_DEV, 128), 0) == iota((CL_DEV, 128), 1)).astype(F32)
        notes[16:32, :] = jnp.sum(number * inner[None], axis=1)
        notes_all[n] = notes[...]

    def tower(c):
        x = feats[rows_of(c), :]
        first = silu(jnp.dot(x, w1[...], preferred_element_type=F32)).astype(BF16)
        second = silu(jnp.dot(first, w2[...], preferred_element_type=F32)).astype(BF16)
        raw = jnp.dot(second, w3[...], preferred_element_type=F32)
        scale = lax.rsqrt(jnp.mean(raw * raw, axis=1, keepdims=True) + 1e-06)
        embedding = (raw * scale * gain_ref[...]).astype(BF16)
        for j in range(NARROW):
            emb[j, rows_of(c), :] = embedding[:, j * PIECE : (j + 1) * PIECE]
        rhs[landing(c, n), 0:128] = emb[n, rows_of(c), :]

    def send_rows(c):
        loop(1, NARROW, lambda d: emb_copy(c, d).start())

    def place_rows():
        loop(1, NARROW, lambda d: notes_copy(d).wait_recv())
        earlier = [jnp.zeros((WIDE, 128), F32)]
        for m in range(NARROW - 1):
            earlier.append(earlier[m] + notes_all[m, 16:32, :])
        earlier = [number.astype(BF16) for number in earlier]
        inside_level = iota((128, 128), 0).astype(F32)
        owner_level = iota((WIDE, 128), 0).astype(F32)
        cap = float(CAP)

        def place_chunk(c, before):
            held = []
            for m in range(NARROW):
                for part in range(PARTS):
                    k = PARTS * c + part
                    row = notes_all[m, pl.ds(k, 1), :]
                    owner = jnp.floor(row * (1.0 / CL_DEV))
                    held.append(jnp.where(owner_level == owner, 1.0, 0.0))
                    inside = jnp.where(inside_level == row - owner * CL_DEV, 1.0, 0.0).astype(BF16)
                    ahead = jnp.dot(earlier[m], inside, preferred_element_type=F32) * held[-1]
                    rank_all[m, pl.ds(k, 1), :] = notes_all[m, pl.ds(8 + k, 1), :] + jnp.sum(
                        ahead, axis=0, keepdims=True
                    )
            ordered = jnp.dot(jnp.concatenate(held, axis=0).astype(BF16), sums, preferred_element_type=F32)
            carry = jnp.zeros((WIDE, 128), F32)
            for q in range(NARROW * PARTS):
                spot = ordered[WIDE * q : WIDE * (q + 1), :128] + carry - 1.0
                spot = jnp.where(held[q] > 0.0, spot, -1.0)
                dest[NARROW * PARTS * c + q] = spot
                dest_over[NARROW * PARTS * c + q] = jnp.where(spot >= cap, spot - cap + before, -1.0)
                carry = carry + ordered[WIDE * q : WIDE * (q + 1), 128:]
            return before + jnp.maximum(carry - cap, 0.0)

        before = lax.fori_loop(0, CHUNKS, place_chunk, jnp.zeros((WIDE, 128), F32))
        most = jnp.max(before, axis=0, keepdims=True)
        spill[...] = jnp.broadcast_to(jnp.where(most > float(OVER), 1.0, 0.0), spill.shape)

        ranks = rank_all[...].reshape(BLOCKS, 128)
        turned = jnp.transpose(jnp.concatenate([ranks, jnp.zeros((128 - BLOCKS, 128), F32)], axis=0))
        left = iota((128, 128), 1) < 64

        def tag_chunk(c):
            moved = pltpu.roll(turned, (128 - PARTS * c) % 128, 1)
            for m in range(NARROW):
                for part in range(PARTS):
                    at = 8 * m + part
                    column = jnp.broadcast_to(moved[:, at : at + 1], (128, 128))
                    high = jnp.floor(column * (1.0 / 32.0)) * 32.0
                    rows = pl.ds(pl.multiple_of((NARROW * c + m) * CHUNK + part * 128, 128), 128)
                    rhs[rows, 128:256] = jnp.where(left, high, column - high).astype(BF16)

        loop(0, CHUNKS, tag_chunk)

    def spread_queries():
        loop(0, WIDE - 1, lambda i: q_wide_copy(peer_step(i)).wait_recv())
        at = iota((4 * WIDE, 8 * WIDE), 0)
        pick = iota((4 * WIDE, 8 * WIDE), 1) == at // 4 * 8 + at % 4
        spread = q_wide[...].reshape(8 * WIDE, PIECE).astype(BF16)
        q_mine[...] = jnp.dot(pick.astype(F32).astype(BF16), spread, preferred_element_type=F32).astype(BF16)
        q_all[n] = q_mine[...]
        loop(1, NARROW, lambda d: q_narrow_copy(d).start())

    def write_tag(k, g, tag, cap):
        tag = tag + pltpu.roll(tag, 64, 1)
        for half in range(2):
            size = min(cap - 128 * half, 128)
            if size > 0:
                eye = iota((size, 128), 0) == iota((size, 128), 1)
                line = jnp.sum(jnp.where(eye, tag[128 * half : 128 * half + size], 0.0), axis=0, keepdims=True)
            else:
                line = spill[0:1, :]
            tag_out[k, g, half : half + 1, :] = line

    def send_group(k, g, last=False):
        @pl.when(k != SELF)
        def _():
            data_copy(g, k, last).start()
            tag_copy(g, k).start()

        @pl.when(k == SELF)
        def _():
            own_data(g, last).start()
            own_tag(g).start()

    def pack(c):
        loop(1, NARROW, lambda d: emb_copy(c, d).wait_recv())
        blocks = NARROW * PARTS
        both = CAP + OVER
        spot = iota((CAP, 128), 0).astype(F32)
        spot_over = iota((OVER, 128), 0).astype(F32)

        def to_owners(i):
            lines = []
            for j in range(BATCH):
                to = wide_peer(BATCH * i + j)
                for spots, level in ((dest, spot), (dest_over, spot_over)):
                    parts = []
                    for q in range(blocks):
                        row = spots[blocks * c + q, pl.ds(to, 1), :]
                        parts.append(jnp.where(level == row, 1.0, 0.0).astype(BF16))
                    lines.append(jnp.concatenate(parts, axis=1))
            onehot = jnp.concatenate(lines, axis=0)
            source = rhs[pl.ds(pl.multiple_of(c * (NARROW * CHUNK), NARROW * CHUNK), NARROW * CHUNK), :]
            packed = jnp.dot(onehot, source, preferred_element_type=F32)
            for j in range(BATCH):
                k = BATCH * i + j
                main = packed[both * j : both * j + CAP]
                stage[k, packed_rows(c), :] = main[:, :128].astype(BF16)
                write_tag(k, c, main[:, 128:], CAP)
                send_group(k, c)
                over_sum[k] += packed[both * j + CAP : both * (j + 1)]

        loop(0, WIDE // BATCH, to_owners)

    def pack_over():
        def to_owner(k):
            rest = over_sum[k]
            stage[k, packed_rows(CHUNKS, True), :] = rest[:, :128].astype(BF16)
            write_tag(k, CHUNKS, rest[:, 128:], OVER)
            send_group(k, CHUNKS, True)

        loop(0, WIDE, to_owner)

    def local_best():
        loop(1, NARROW, lambda d: q_narrow_copy(d).wait_recv())
        score = jnp.zeros((4 * WIDE, ROWS), F32)
        for j in range(NARROW):
            score += lax.dot_general(q_all[j], emb[j], NT, preferred_element_type=F32)
        ids_f = ids_ref[...].astype(F32)
        id_row = jnp.concatenate([ids_f[k : k + 1, :] for k in range(8)], axis=1)
        key_row = id_row * float(ROWS) + iota((1, ROWS), 1).astype(F32)
        eye = iota((128, 128), 0) == iota((128, 128), 1)
        order = iota((128, ROWS), 1).astype(F32)
        for k in range(8):
            key = jnp.sum(jnp.where(eye, key_row[:, k * 128 : (k + 1) * 128], 0.0), axis=1, keepdims=True)
            position = jnp.sum(jnp.where(key_row < key, 1.0, 0.0), axis=1, keepdims=True)
            perm[k * 128 : (k + 1) * 128, :] = jnp.where(order == position, 1.0, 0.0).astype(BF16)
        high = score.astype(BF16)
        low = (score - high.astype(F32)).astype(BF16)
        id_high = jnp.floor(id_row * (1.0 / 32.0)) * 32.0
        line = iota((16, ROWS), 0)
        extra = jnp.where(line == 0, id_high, jnp.where(line == 1, id_row - id_high, 0.0)).astype(BF16)
        arranged = jnp.dot(jnp.concatenate([high, low, extra], axis=0), perm[...], preferred_element_type=F32)
        top = arranged[0:64] + arranged[64:128]
        seg = jnp.broadcast_to(arranged[128:129] + arranged[129:130], (8, ROWS))
        lane = iota((8, ROWS), 1)
        for step in (1, 2, 4, 8, 16):
            same = (pltpu.roll(seg, step, 1) == seg) & (lane >= step)
            gate = jnp.where(same, 0.0, -jnp.inf)[0:1]
            top = jnp.maximum(top, pltpu.roll(top, step, 1) + gate)
        closing = (pltpu.roll(seg, ROWS - 1, 1) != seg) | (lane == ROWS - 1)
        end_id = jnp.where(closing, seg, -1.0)[0:1]
        for k in range(ROWS // 128):
            match = owner_of[...].astype(F32) == end_id[:, k * 128 : (k + 1) * 128]
            ends[:, k * 128 : (k + 1) * 128] = jnp.where(match, 1.0, 0.0).astype(BF16)
        high = top.astype(BF16)
        low = (top - high.astype(F32)).astype(BF16)
        ones = jnp.ones((16, ROWS), BF16)
        found = lax.dot_general(jnp.concatenate([high, low, ones], axis=0), ends[...], NT, preferred_element_type=F32)
        by_slot = jnp.where(found[128:129] > 0.0, found[0:64] + found[64:128], -jnp.inf)
        for j in range(NARROW):
            table[j] = by_slot[8 * j : 8 * j + 8]
        table_in[n] = table[n]
        loop(1, NARROW, lambda d: table_copy(d).start())

    def merge_narrow():
        loop(1, NARROW, lambda d: table_copy(d).wait_recv())
        merged = jnp.max(table_in[...], axis=0)
        for o in range(WIDE):
            group = merged[:, o // 4 * 128 : o // 4 * 128 + 128]
            final[o] = pltpu.roll(group, (128 - 32 * (o % 4)) % 128, 1) if o % 4 else group
        final_in[w] = final[w]
        loop(0, WIDE - 1, lambda i: final_copy(peer_step(i)).start())

    def merge_wide():
        loop(0, WIDE - 1, lambda i: final_copy(peer_step(i)).wait_recv())
        best_ref[...] = jnp.max(final_in[...], axis=0)

    over_sum[...] = jnp.zeros_like(over_sum)
    note_rows()
    for group in [feat_loads] + weight_loads:
        for copy in group:
            copy.wait()

    def turn(t):
        @pl.when(t < CHUNKS)
        def _():
            tower(t)

        @pl.when(t == 0)
        def _():
            pl.semaphore_wait(barrier, NARROW - 1 + WIDE - 1)
            loop(1, NARROW, lambda d: notes_copy(d).start())

        @pl.when(t < CHUNKS)
        def _():
            send_rows(t)

        @pl.when(t == 0)
        def _():
            loop(0, WIDE - 1, lambda i: q_wide_copy(peer_step(i)).start())

        @pl.when(t == 1)
        def _():
            place_rows()

        @pl.when(t == 2)
        def _():
            spread_queries()

        @pl.when(t == CHUNKS)
        def _():
            local_best()

        @pl.when(t >= 1)
        def _():
            pack(t - 1)

    loop(0, CHUNKS + 1, turn)
    pack_over()
    merge_narrow()
    merge_wide()

    def settle_wide(i):
        k = peer_step(i)
        q_wide_copy(k).wait_send()
        final_copy(k).wait_send()

    def settle_narrow(d):
        notes_copy(d).wait_send()
        q_narrow_copy(d).wait_send()
        table_copy(d).wait_send()

    loop(0, WIDE - 1, settle_wide)
    loop(1, NARROW, settle_narrow)

    def settle_chunk(c):
        loop(1, NARROW, lambda d: emb_copy(c, d).wait_send())
        settle_group(c, False)

    def settle_group(g, last):
        def settle(i):
            data_copy(g, peer_step(i), last).wait()
            tag_copy(g, peer_step(i)).wait()

        loop(0, WIDE - 1, settle)
        own_data(g, last).wait()
        own_tag(g).wait()

    loop(0, CHUNKS, settle_chunk)
    settle_group(CHUNKS, True)


def run_exchange(features, w_first, w_second, w_third, gain, ids, slots, queries):
    vmem = pl.BlockSpec(memory_space=pltpu.VMEM)
    anywhere = pl.BlockSpec(memory_space=pl.ANY)
    dma = pltpu.SemaphoreType.DMA
    return pl.pallas_call(
        exchange,
        out_shape=(
            jax.ShapeDtypeStruct((WIDE, TOTAL, PIECE), BF16),
            jax.ShapeDtypeStruct((WIDE, GROUPS, 2, 128), F32),
            jax.ShapeDtypeStruct((8, 128), F32),
        ),
        in_specs=[anywhere] * 4 + [vmem] * 4,
        out_specs=(anywhere, anywhere, vmem),
        scratch_shapes=[
            pltpu.VMEM((ROWS, 1024), BF16),
            pltpu.VMEM((1024, 1024), BF16),
            pltpu.VMEM((1024, 1024), BF16),
            pltpu.VMEM((1024, 1024), BF16),
            pltpu.VMEM((NARROW, ROWS, PIECE), BF16),
            pltpu.VMEM((NARROW * ROWS, 256), BF16),
            pltpu.VMEM((WIDE, TOTAL, PIECE), BF16),
            pltpu.VMEM((WIDE, GROUPS, 2, 128), F32),
            pltpu.VMEM((32, 128), F32),
            pltpu.VMEM((NARROW, 32, 128), F32),
            pltpu.VMEM((NARROW, 8, 128), F32),
            pltpu.VMEM((SLOTS, 128), jnp.int32),
            pltpu.VMEM((SLOTS, 128), F32),
            pltpu.VMEM((BLOCKS, WIDE, 128), F32),
            pltpu.VMEM((BLOCKS, WIDE, 128), F32),
            pltpu.VMEM((8, 128), F32),
            pltpu.VMEM((WIDE, OVER, 256), F32),
            pltpu.VMEM((WIDE, 8, PIECE), F32),
            pltpu.VMEM((4 * WIDE, PIECE), BF16),
            pltpu.VMEM((NARROW, 4 * WIDE, PIECE), BF16),
            pltpu.VMEM((ROWS, ROWS), BF16),
            pltpu.VMEM((SLOTS, ROWS), BF16),
            pltpu.VMEM((NARROW, 8, SLOTS), F32),
            pltpu.VMEM((NARROW, 8, SLOTS), F32),
            pltpu.VMEM((WIDE, 8, 128), F32),
            pltpu.VMEM((WIDE, 8, 128), F32),
            dma((4, 4)),
            dma((NARROW,)), dma((NARROW,)),
            dma((WIDE,)), dma((WIDE,)),
            dma((NARROW,)), dma((NARROW,)),
            dma((CHUNKS, NARROW)), dma((CHUNKS, NARROW)),
            dma((GROUPS, WIDE)), dma((GROUPS, WIDE)),
            dma((GROUPS, WIDE)), dma((GROUPS, WIDE)),
            dma((NARROW,)), dma((NARROW,)),
            dma((WIDE,)), dma((WIDE,)),
            dma((GROUPS,)), dma((GROUPS,)),
        ],
        compiler_params=pltpu.CompilerParams(
            collective_id=0, has_side_effects=True, vmem_limit_bytes=56 * 2**20
        ),
        name="exchange",
    )(features, w_first, w_second, w_third, gain, ids, slots, queries)


def unpack(arrived_ref, tags_ref, slab_ref):
    spot = iota((256, TOTAL), 0).astype(F32).astype(BF16)
    for i in range(4):
        parts = []
        for g in range(GROUPS):
            for half in range(2):
                size = min((CAP if g < CHUNKS else OVER) - 128 * half, 128)
                if size > 0:
                    parts.append(tags_ref[i, g, half : half + 1, :size])
        row = jnp.concatenate(parts, axis=1) - 1.0
        for t in range(CL_DEV * MOST // 256):
            line = jnp.broadcast_to(row - 256.0 * t, (16, TOTAL)).astype(BF16)
            line = jnp.concatenate([line] * 16, axis=0)
            onehot = jnp.where(spot == line, jnp.ones_like(line), jnp.zeros_like(line))
            slab_ref[i, t * 256 : (t + 1) * 256, :] = jnp.dot(
                onehot, arrived_ref[i], preferred_element_type=F32
            ).astype(BF16)


def run_unpack(arrived, tags):
    return pl.pallas_call(
        unpack,
        grid=(WIDE // 4,),
        out_shape=jax.ShapeDtypeStruct((WIDE, CL_DEV * MOST, PIECE), BF16),
        in_specs=[
            pl.BlockSpec((4, TOTAL, PIECE), lambda b: (b, 0, 0)),
            pl.BlockSpec((4, GROUPS, 2, 128), lambda b: (b, 0, 0, 0)),
        ],
        out_specs=pl.BlockSpec((4, CL_DEV * MOST, PIECE), lambda b: (b, 0, 0)),
        compiler_params=pltpu.CompilerParams(vmem_limit_bytes=32 * 2**20),
        name="unpack",
    )(arrived, tags)


def pass_on(in_ref, out_ref):
    out_ref[...] = in_ref[...]


def run_pass_on(slab):
    block = pl.BlockSpec((1, CL_DEV * MOST, PIECE), lambda b: (b, 0, 0))
    return pl.pallas_call(
        pass_on,
        grid=(WIDE,),
        out_shape=jax.ShapeDtypeStruct(slab.shape, slab.dtype),
        in_specs=[block],
        out_specs=block,
        name="pass_on",
    )(slab)


def slot_table(id_list, cluster_slots, total):
    levels = jnp.arange(total, dtype=jnp.int32)
    onehot = (id_list[:, None] == levels[None, :]).astype(jnp.bfloat16)
    high_part = (cluster_slots // 64).astype(jnp.bfloat16)
    low_part = (cluster_slots % 64).astype(jnp.bfloat16)
    slot_value = 64.0 * jnp.dot(onehot, high_part, preferred_element_type=jnp.float32) + jnp.dot(
        onehot, low_part, preferred_element_type=jnp.float32
    )
    return (onehot, slot_value.astype(jnp.int32))


def cluster_ranks(onehot):
    count, total = onehot.shape
    block = math.gcd(count, 256)
    number = count // block
    stacked = onehot.reshape(number, block, total)
    inner = jnp.arange(block, dtype=jnp.int32)
    lower = (inner[:, None] >= inner[None, :]).astype(jnp.bfloat16)
    inside = jnp.einsum("rs,bsc->brc", lower, stacked, preferred_element_type=jnp.float32)
    block_sums = inside[:, -1, :]
    outer = jnp.arange(number, dtype=jnp.int32)
    before = (outer[:, None] > outer[None, :]).astype(jnp.float32)
    earlier = jnp.dot(
        before, block_sums, precision=lax.Precision.HIGHEST, preferred_element_type=jnp.float32
    )
    position = jnp.sum(stacked * (inside - 1.0 + earlier[:, None, :]), axis=2)
    return (position.reshape(count).astype(jnp.int32), jnp.sum(block_sums, axis=0))


def padded_slab(features, cluster_ids, cluster_slots, w_first, w_second, w_third, emb_gain):
    first = jax.nn.silu(jnp.dot(features, w_first, preferred_element_type=F32)).astype(BF16)
    second = jax.nn.silu(jnp.dot(first, w_second, preferred_element_type=F32)).astype(BF16)
    raw = jnp.dot(second, w_third, preferred_element_type=F32)
    scale = lax.rsqrt(jnp.mean(raw * raw, axis=1, keepdims=True) + 1e-06)
    embedding = (raw * scale * emb_gain).astype(BF16)
    block_ids = lax.all_gather(cluster_ids[:, 0], "narrow", axis=0, tiled=True)
    block_rows = block_ids.shape[0]
    onehot, slot_of = slot_table(block_ids, cluster_slots, SLOTS)
    positions, _ = cluster_ranks(onehot)
    flat_slot = slot_of * MOST + positions
    sliced = lax.all_to_all(embedding, "narrow", split_axis=1, concat_axis=0, tiled=True)
    source = (
        jnp.full((SLOTS * MOST,), block_rows, jnp.int32)
        .at[flat_slot]
        .set(jnp.arange(block_rows, dtype=jnp.int32))
    )
    padded = jnp.concatenate([sliced, jnp.zeros((1, PIECE), BF16)], axis=0)
    outgoing = jnp.take(padded, source, axis=0).reshape(WIDE, CL_DEV * MOST, PIECE)
    return run_pass_on(lax.all_to_all(outgoing, "wide", split_axis=0, concat_axis=0, tiled=True))


def shards(features, cluster_ids, cluster_slots, w_first, w_second, w_third, emb_gain, queries):
    ids = cluster_ids.reshape(8, 128)
    query = jnp.pad(queries.astype(F32), ((0, 4), (0, 0)))
    arrived, tags, best = run_exchange(
        features, w_first, w_second, w_third, emb_gain.reshape(1, 1024), ids, cluster_slots.reshape(1, SLOTS), query
    )
    fits = jnp.max(tags[:, CHUNKS, 1, 0]) == 0.0
    slab = lax.cond(
        fits,
        lambda: run_unpack(arrived, tags),
        lambda: padded_slab(features, cluster_ids, cluster_slots, w_first, w_second, w_third, emb_gain),
    )
    return (best[:, :CL_DEV], slab.reshape(WIDE, CL_DEV, MOST, PIECE))


def solution(mesh):
    placed = (
        P(("wide", "narrow"), None),
        P(("wide", "narrow"), None),
        P(),
        P(),
        P(),
        P(),
        P(),
        P("wide", "narrow"),
    )
    return jax.shard_map(
        shards,
        mesh=mesh,
        in_specs=placed,
        out_specs=(P("narrow", "wide"), P(None, "wide", None, "narrow")),
        check_vma=False,
    )
```
